32 devices in a mesh: row: 4 (over y, x), col: 8 (over z, core).
Axes of the slice: x: 2, y: 2, z: 4, core: 2. Of those that a mesh axis runs over, the one named last changes fastest.
Arguments:
- vectors: bfloat16 [16, 16384], P(None, ('row', 'col')), may hold values from -6 to 6
- blocks: bfloat16 [4, 1536, 128, 128], P('row', 'col'), may hold values from -0.09375 to 0.09375
- row_ptr: int32 [4, 264], P('row', 'col'), may hold values from 0 to 192, as said below
- col_idx: int32 [4, 1536], P('row', 'col'), may hold values from 0 to 15, as said below
Outputs:
- product: float32 [16, 16384], P(None, ('row', 'col'))
The draws below stay inside these ranges and needn't reach their ends.
Inputs may be any that keep to these rules, and one draw needn't show every extreme that they name: For each tile, row_ptr starts at 0, never falls, and ends at the tile's count of live slots; at least one tile has exactly 192 live slots in every draw, and counts differ strongly from tile to tile. `col_idx`: within each block row of a tile the live slots name strictly rising block columns, so no block position of a tile is stored twice; slots at or past a tile's count hold a valid column and are unused.
All inputs are finite; a program needn't handle non-finite values.
Results may differ from the reference program's by a relative error of at most 0.0003.
Values may be sent and summed in bfloat16 or wider, within the bound.
A program may use at most 64 MiB of HBM per device.

```python
import jax
import jax.numpy as jnp
from jax import lax

BLOCK = 128
VECTORS = 16
SEG_BLOCKS = 4
CAPACITY = 192
TILE_ROWS = 32
TILE_COLS = 16
ORDER = 16384
SLOTS = 1536
N_ROW = 4
N_COL = 8


def tile_layout(key):
    base = jax.random.fold_in(key, 11)
    tile_count = N_ROW * N_COL
    spots = TILE_ROWS * TILE_COLS
    keys = jax.random.split(base, 3)
    raw_draw = jax.random.randint(keys[0], (tile_count,), 1, CAPACITY + 1)
    counts = jnp.maximum(raw_draw * raw_draw // CAPACITY, 1)
    fullest = jax.random.randint(keys[1], (), 0, tile_count)
    counts = jnp.where(jnp.arange(tile_count) == fullest, CAPACITY, counts)
    perm_keys = jax.random.split(keys[2], tile_count)
    chosen = jax.vmap(lambda one_key: jax.random.permutation(one_key, spots))(perm_keys)[:, :CAPACITY]
    slot_ids = jnp.arange(CAPACITY)
    keyed = jnp.where(slot_ids[None, :] < counts[:, None], chosen, chosen + spots)
    ordered = jnp.sort(keyed, axis=1)
    live_slots = ordered < spots
    position = ordered % spots
    block_rows = position // TILE_COLS
    block_cols = position % TILE_COLS
    edges = jnp.arange(TILE_ROWS + 1)
    below = live_slots[:, :, None] & (block_rows[:, :, None] < edges[None, None, :])
    pointers = jnp.sum(below.astype(jnp.int32), axis=1)
    return (pointers.reshape(N_ROW, N_COL * (TILE_ROWS + 1)).astype(jnp.int32), block_cols.reshape(N_ROW, N_COL * CAPACITY).astype(jnp.int32))


def draw_row_ptr(key, part):
    return tile_layout(key)[0]


def draw_col_idx(key, part):
    return tile_layout(key)[1]


def level_of(rng, shape, pieces, smallest, top_value):
    factor_of, own = 1.0, jax.random.fold_in(rng, 6)
    for dim, blocks in pieces:
        heights = jnp.exp(jax.random.uniform(jax.random.fold_in(own, dim), (blocks,), jnp.float32, smallest / len(pieces), top_value / len(pieces)))
        factor_of = factor_of * jnp.repeat(heights, shape[dim] // blocks).reshape([-1 if axis == dim else 1 for axis in range(len(shape))])
    return factor_of


def scatter_about(own_key, dims, deviation, bound, cuts=(), held_as=jnp.bfloat16):
    entries = jax.random.normal(own_key, dims, jnp.float32) * deviation
    if len(cuts) > 0:
        entries = level_of(own_key, dims, cuts, -0.22, 0.18) * entries
    return jnp.clip(entries, min=-bound, max=bound).astype(held_as)


def setup_inputs(seed: int = 0) -> dict:
    key_list = jax.random.split(jax.random.key(seed), 5)
    return {
        "vectors": scatter_about(key_list[0], (VECTORS, ORDER), 1.0, 6.0, ((1, 32),)),
        "blocks": scatter_about(key_list[1], (N_ROW, SLOTS, BLOCK, BLOCK), (2 * CAPACITY * BLOCK // (3 * SEG_BLOCKS)) ** -0.5, 0.09375, ((0, 4), (1, 8))),
        "row_ptr": draw_row_ptr(jax.random.fold_in(key_list[4], 71), 0),
        "col_idx": draw_col_idx(jax.random.fold_in(key_list[4], 71), 0),
    }


def tile_terms(row_side, col_side, tile_blocks, pointers, columns):
    slot_ids = jnp.arange(tile_blocks.shape[0], dtype=jnp.int32)
    live_slots = slot_ids < pointers[-1]
    slot_rows = jnp.sum((slot_ids[:, None] >= pointers[None, 1:]).astype(jnp.int32), axis=1)
    slot_rows = jnp.minimum(slot_rows, pointers.shape[0] - 2).astype(jnp.int32)
    count_vectors = row_side.shape[0]
    edge = tile_blocks.shape[1]
    row_blocks = row_side.reshape(count_vectors, -1, edge)
    col_blocks = col_side.reshape(count_vectors, -1, edge)
    picked_rows = jnp.take(row_blocks, slot_rows, axis=1).astype(jnp.float32)
    picked_cols = jnp.take(col_blocks, columns, axis=1).astype(jnp.float32)
    widened = tile_blocks.astype(jnp.float32)
    forward = jnp.einsum("ksj,sij->ski", picked_cols, widened)
    backward = jnp.einsum("ksi,sij->skj", picked_rows, widened)
    live_mask = live_slots[:, None, None]
    forward = jnp.where(live_mask, forward, jnp.zeros_like(forward))
    backward = jnp.where(live_mask, backward, jnp.zeros_like(backward))
    forward_sum = jax.ops.segment_sum(forward, slot_rows, num_segments=row_blocks.shape[1])
    backward_sum = jax.ops.segment_sum(backward, columns, num_segments=col_blocks.shape[1])
    return forward_sum, backward_sum


def reference(vectors, blocks, row_ptr, col_idx):
    count_vectors = vectors.shape[0]
    segment = vectors.shape[1] // (N_ROW * N_COL)
    by_segment = vectors.reshape(count_vectors, N_ROW, N_COL, segment)
    tile_blocks = blocks.reshape(N_ROW, N_COL, -1, BLOCK, BLOCK)
    pointers = row_ptr.reshape(N_ROW, N_COL, -1)
    columns = col_idx.reshape(N_ROW, N_COL, -1)

    def advance(carry, index):
        forward_total, backward_total = carry
        row_at = index // N_COL
        col_at = index % N_COL
        row_side = lax.dynamic_index_in_dim(by_segment, row_at, 1, keepdims=False).reshape(count_vectors, -1)
        col_side = lax.dynamic_index_in_dim(by_segment, col_at, 2, keepdims=False).reshape(count_vectors, -1)
        forward_sum, backward_sum = tile_terms(row_side, col_side, tile_blocks[row_at, col_at], pointers[row_at, col_at], columns[row_at, col_at])
        forward_total = forward_total.at[row_at].add(forward_sum)
        backward_total = backward_total.at[col_at].add(backward_sum)
        return (forward_total, backward_total), None

    start = (jnp.zeros((N_ROW, TILE_ROWS, count_vectors, BLOCK), jnp.float32), jnp.zeros((N_COL, TILE_COLS, count_vectors, BLOCK), jnp.float32))
    (forward_total, backward_total), _ = lax.scan(advance, start, jnp.arange(N_ROW * N_COL, dtype=jnp.int32))
    forward_parts = forward_total.reshape(N_ROW * N_COL, SEG_BLOCKS, count_vectors, BLOCK)
    backward_parts = backward_total.reshape(N_COL, N_ROW, SEG_BLOCKS, count_vectors, BLOCK).transpose(1, 0, 2, 3, 4).reshape(N_ROW * N_COL, SEG_BLOCKS, count_vectors, BLOCK)
    combined = forward_parts + backward_parts
    return combined.transpose(2, 0, 1, 3).reshape(count_vectors, -1)
```

```python
import functools

import jax
import jax.numpy as jnp
from jax import lax
from jax.experimental import pallas as pl
from jax.experimental.pallas import tpu as pltpu
from jax.sharding import PartitionSpec as P

MESH = pl.DeviceIdType.MESH
GROUP = 16
FAR = 1 << 20


def slot_tables(pointers, columns, tile_cols):
    slots = columns.shape[1]
    tile_rows = pointers.shape[1] - 1
    i32 = jnp.int32

    def iota(shape, dim):
        return lax.broadcasted_iota(i32, shape, dim)

    def total(mask_or_value, axis):
        return jnp.sum(mask_or_value, axis=axis, keepdims=True)

    def count(mask, axis):
        return total(jnp.where(mask, 1, 0), axis)

    edge = (tile_rows + 1, tile_rows + 1)
    pointer_col = total(jnp.where(iota(edge, 0) == iota(edge, 1), pointers, 0), 1)
    wide = (tile_rows + 1, slots)
    rows = count(pointer_col <= iota(wide, 1), 0) - 1
    keep_row = jnp.where(count(pointer_col == iota(wide, 1), 0) == 0, 1, 0)

    square = (slots, slots)
    lane, sub = iota(square, 1), iota(square, 0)
    slot_row = iota((1, slots), 1)
    key = jnp.where(rows < tile_rows, columns * slots, FAR) + slot_row
    rows = jnp.minimum(rows, tile_rows - 1)
    same = lane == sub
    key_col = total(jnp.where(same, key, 0), 1)
    rows_col = total(jnp.where(same, rows, 0), 1)
    rank_col = count(key < key_col, 1)
    chosen = rank_col == lane
    order = total(jnp.where(chosen, sub, 0), 0)
    order_rows = total(jnp.where(chosen, rows_col, 0), 0)
    tall = (tile_cols, slots)
    ends_col = count(key < (iota(tall, 0) + 1) * slots, 1)
    starts = count(ends_col == iota(tall, 1), 0)
    keep_col = jnp.where((starts == 0) & (slot_row > 0), 1, 0)
    side = (tile_cols, tile_cols)
    ends = total(jnp.where(iota(side, 0) == iota(side, 1), ends_col, 0), 0)
    return keep_row, order, order_rows, keep_col, ends


def kernel(
    n_row, n_col, chunks,
    vec_hbm, blk_hbm, ptr_hbm, col_hbm, out_ref,
    vec, blk, ptr_s, col_s, ptr_v, col_v, table_v, table_s,
    row_side, col_side, run, fwd, bwd, near, fwd_in, bwd_in,
    vec_sem, blk_sem, idx_sem,
    rs_send, rs_recv, cs_send, cs_recv, near_send, near_recv,
    f_send, f_recv, b_send, b_recv,
):
    r = lax.axis_index("row")
    c = lax.axis_index("col")
    z, core = c // 2, c % 2
    nz = n_col // 2
    seg = vec.shape[1] // 128
    slots = blk.shape[0]
    per = slots // chunks
    f32 = jnp.float32

    get_vec = pltpu.make_async_copy(vec_hbm, vec, vec_sem)
    get_vec.start()
    index_copies = [
        pltpu.make_async_copy(src, dst, idx_sem.at[k])
        for k, (src, dst) in enumerate(
            ((ptr_hbm, ptr_v), (col_hbm, col_v), (ptr_hbm, ptr_s), (col_hbm, col_s))
        )
    ]
    for copy in index_copies:
        copy.start()

    def chunk_copy(k):
        part = pl.ds(k * per, per)
        return pltpu.make_async_copy(blk_hbm.at[0, part], blk.at[part], blk_sem.at[k])

    for k in range(chunks):
        chunk_copy(k).start()

    barrier = pltpu.get_barrier_semaphore()

    @pl.loop(1, n_row)
    def _(d):
        pl.semaphore_signal(barrier, inc=1, device_id=((r + d) % n_row, c), device_id_type=MESH)

    @pl.loop(1, n_col)
    def _(d):
        pl.semaphore_signal(barrier, inc=1, device_id=(r, (c + d) % n_col), device_id_type=MESH)

    get_vec.wait()
    for u in range(seg):
        piece = vec[:, u * 128:(u + 1) * 128]
        row_side[c * seg + u] = piece
        col_side[r * seg + u] = piece
    pl.semaphore_wait(barrier, n_row + n_col - 2)

    def cs_copy(d, mine):
        owner = r if mine else (r + n_row - d) % n_row
        part = pl.ds(owner * seg, seg)
        return pltpu.make_async_remote_copy(
            src_ref=col_side.at[part], dst_ref=col_side.at[part],
            send_sem=cs_send.at[d], recv_sem=cs_recv.at[d],
            device_id=((r + d) % n_row, c), device_id_type=MESH)

    def rs_copy(d, mine):
        owner = c if mine else (c + n_col - d) % n_col
        part = pl.ds(owner * seg, seg)
        return pltpu.make_async_remote_copy(
            src_ref=row_side.at[part], dst_ref=row_side.at[part],
            send_sem=rs_send.at[d], recv_sem=rs_recv.at[d],
            device_id=(r, (c + d) % n_col), device_id_type=MESH)

    @pl.loop(1, n_row)
    def _(d):
        cs_copy(d, True).start()

    @pl.loop(1, n_col)
    def _(d):
        rs_copy(d, True).start()

    for copy in index_copies:
        copy.wait()
    table_v[...] = jnp.zeros_like(table_v)
    tables = slot_tables(ptr_v[...], col_v[...], n_row * seg)
    for k, entry in enumerate(tables):
        table_v[k:k + 1, 0:entry.shape[1]] = entry
    put_table = pltpu.make_async_copy(table_v, table_s, idx_sem.at[0])
    put_table.start()
    run[slots] = jnp.zeros(run.shape[1:], f32)
    put_table.wait()

    @pl.loop(1, n_row)
    def _(d):
        cs_copy(d, False).wait_recv()

    def forward_group(g, total):
        base = g * GROUP
        sides = [col_side[col_s[0, base + j]] for j in range(GROUP)]
        terms = [
            lax.dot_general(sides[j], blk[base + j], (((1,), (1,)), ((), ())), preferred_element_type=f32)
            for j in range(GROUP)
        ]
        for j in range(GROUP):
            total = total * table_s[0, base + j].astype(f32) + terms[j]
            run[base + j] = total
        return total

    total = jnp.zeros(run.shape[1:], f32)
    for k in range(chunks):
        chunk_copy(k).wait()
        total = lax.fori_loop(k * per // GROUP, (k + 1) * per // GROUP, forward_group, total)

    @pl.loop(0, n_col)
    def _(p):
        for u in range(seg):
            first, last = ptr_s[0, p * seg + u], ptr_s[0, p * seg + u + 1]
            fwd[p % 2, p // 2, u] = run[jnp.where(last > first, last - 1, slots)]

    near_copy = pltpu.make_async_remote_copy(
        src_ref=fwd.at[1 - core], dst_ref=near, send_sem=near_send, recv_sem=near_recv,
        device_id=(r, z * 2 + 1 - core), device_id_type=MESH)
    near_copy.start()

    @pl.loop(1, n_col)
    def _(d):
        rs_copy(d, False).wait_recv()

    def backward_group(g, total):
        base = g * GROUP
        sides = [row_side[table_s[2, base + j]] for j in range(GROUP)]
        terms = [
            lax.dot_general(
                sides[j], blk[table_s[1, base + j]], (((1,), (0,)), ((), ())), preferred_element_type=f32)
            for j in range(GROUP)
        ]
        for j in range(GROUP):
            total = total * table_s[3, base + j].astype(f32) + terms[j]
            run[base + j] = total
        return total

    def f_copy(d, mine):
        to = (z + d) % nz
        return pltpu.make_async_remote_copy(
            src_ref=fwd.at[core, to], dst_ref=fwd_in.at[z if mine else (z + nz - d) % nz],
            send_sem=f_send.at[d], recv_sem=f_recv.at[d],
            device_id=(r, to * 2 + core), device_id_type=MESH)

    groups = slots // GROUP
    early = max(groups // 3, 1)
    total = lax.fori_loop(0, early, backward_group, jnp.zeros(run.shape[1:], f32))
    near_copy.wait()

    @pl.loop(0, nz)
    def _(p):
        fwd[core, p] = fwd[core, p] + near[p]

    @pl.loop(1, nz)
    def _(d):
        f_copy(d, True).start()

    lax.fori_loop(early, groups, backward_group, total)

    @pl.loop(0, n_row)
    def _(p):
        for u in range(seg):
            q = p * seg + u
            last = table_s[4, q]
            first = jnp.where(q > 0, table_s[4, jnp.maximum(q - 1, 0)], 0)
            bwd[p, u] = run[jnp.where(last > first, last - 1, slots)]

    def b_copy(d, mine):
        to = (r + d) % n_row
        return pltpu.make_async_remote_copy(
            src_ref=bwd.at[to], dst_ref=bwd_in.at[r if mine else (r + n_row - d) % n_row],
            send_sem=b_send.at[d], recv_sem=b_recv.at[d],
            device_id=(to, c), device_id_type=MESH)

    @pl.loop(1, n_row)
    def _(d):
        b_copy(d, True).start()

    bwd_in[r] = bwd[r]
    fwd_in[z] = fwd[core, z]

    @pl.loop(1, nz)
    def _(d):
        f_copy(d, False).wait_recv()

    parts = [fwd_in[p] for p in range(nz)]

    @pl.loop(1, n_row)
    def _(d):
        b_copy(d, False).wait_recv()

    parts = parts + [bwd_in[p] for p in range(n_row)]
    result = functools.reduce(lambda a, b: a + b, parts)
    for u in range(seg):
        out_ref[:, u * 128:(u + 1) * 128] = result[u]

    @pl.loop(1, n_row)
    def _(d):
        cs_copy(d, True).wait_send()
        b_copy(d, True).wait_send()

    @pl.loop(1, n_col)
    def _(d):
        rs_copy(d, True).wait_send()

    @pl.loop(1, nz)
    def _(d):
        f_copy(d, True).wait_send()


def body(n_row, n_col, vectors, blocks, row_ptr, col_idx):
    count, segment = vectors.shape
    slots, edge = blocks.shape[1], blocks.shape[2]
    seg = segment // edge
    chunks = 6 if slots % (6 * GROUP) == 0 else 1
    i32, f32, bf16 = jnp.int32, jnp.float32, jnp.bfloat16
    width = -(-max(slots, n_row * seg) // 128) * 128
    nz = n_col // 2
    dma = pltpu.SemaphoreType.DMA
    anywhere = pl.BlockSpec(memory_space=pl.ANY)
    return pl.pallas_call(
        functools.partial(kernel, n_row, n_col, chunks),
        out_shape=jax.ShapeDtypeStruct((count, segment), f32),
        in_specs=[anywhere] * 4,
        out_specs=pl.BlockSpec(memory_space=pltpu.VMEM),
        scratch_shapes=[
            pltpu.VMEM((count, segment), bf16),
            pltpu.VMEM((slots, edge, edge), bf16),
            pltpu.SMEM(row_ptr.shape, i32),
            pltpu.SMEM(col_idx.shape, i32),
            pltpu.VMEM(row_ptr.shape, i32),
            pltpu.VMEM(col_idx.shape, i32),
            pltpu.VMEM((8, width), i32),
            pltpu.SMEM((8, width), i32),
            pltpu.VMEM((n_col * seg, count, edge), bf16),
            pltpu.VMEM((n_row * seg, count, edge), bf16),
            pltpu.VMEM((slots + 1, count, edge), f32),
            pltpu.VMEM((2, nz, seg, count, edge), f32),
            pltpu.VMEM((n_row, seg, count, edge), f32),
            pltpu.VMEM((nz, seg, count, edge), f32),
            pltpu.VMEM((nz, seg, count, edge), f32),
            pltpu.VMEM((n_row, seg, count, edge), f32),
            dma, dma((chunks,)), dma((4,)),
            dma((n_col,)), dma((n_col,)), dma((n_row,)), dma((n_row,)), dma, dma,
            dma((nz,)), dma((nz,)), dma((n_row,)), dma((n_row,)),
        ],
        compiler_params=pltpu.CompilerParams(
            collective_id=0, has_side_effects=True, vmem_limit_bytes=40 * 1024 * 1024),
        cost_estimate=pl.CostEstimate(
            flops=4 * slots * count * edge * edge, bytes_accessed=2 * slots * edge * edge, transcendentals=0),
    )(vectors, blocks, row_ptr, col_idx)


def solution(mesh):
    in_specs = (
        P(None, ("row", "col")),
        P("row", "col", None, None),
        P("row", "col"),
        P("row", "col"),
    )
    out_specs = P(None, ("row", "col"))
    shape = dict(mesh.shape)
    return jax.shard_map(
        functools.partial(body, shape["row"], shape["col"]),
        mesh=mesh, in_specs=in_specs, out_specs=out_specs, check_vma=False)
```

```python
import functools
import math

import jax
import jax.numpy as jnp
from jax import lax
from jax.experimental import pallas as pl
from jax.experimental.pallas import tpu as pltpu
from jax.sharding import PartitionSpec as P

MESH = pl.DeviceIdType.MESH
GROUP = 48
FAR = 1 << 20


def slot_tables(pointers, columns, tile_cols):
    slots = columns.shape[1]
    tile_rows = pointers.shape[1] - 1
    i32 = jnp.int32

    def iota(shape, dim):
        return lax.broadcasted_iota(i32, shape, dim)

    def total(mask_or_value, axis):
        return jnp.sum(mask_or_value, axis=axis, keepdims=True)

    def count(mask, axis):
        return total(jnp.where(mask, 1, 0), axis)

    edge = (tile_rows + 1, tile_rows + 1)
    pointer_col = total(jnp.where(iota(edge, 0) == iota(edge, 1), pointers, 0), 1)
    wide = (tile_rows + 1, slots)
    rows = count(pointer_col <= iota(wide, 1), 0) - 1
    keep_row = jnp.where(count(pointer_col == iota(wide, 1), 0) == 0, 1, 0)

    square = (slots, slots)
    lane, sub = iota(square, 1), iota(square, 0)
    slot_row = iota((1, slots), 1)
    key = jnp.where(rows < tile_rows, columns * slots, FAR) + slot_row
    rows = jnp.minimum(rows, tile_rows - 1)
    same = lane == sub
    key_col = total(jnp.where(same, key, 0), 1)
    rows_col = total(jnp.where(same, rows, 0), 1)
    rank_col = count(key < key_col, 1)
    chosen = rank_col == lane
    order = total(jnp.where(chosen, sub, 0), 0)
    order_rows = total(jnp.where(chosen, rows_col, 0), 0)
    tall = (tile_cols, slots)
    ends_col = count(key < (iota(tall, 0) + 1) * slots, 1)
    starts = count(ends_col == iota(tall, 1), 0)
    keep_col = jnp.where((starts == 0) & (slot_row > 0), 1, 0)
    side = (tile_cols, tile_cols)
    ends = total(jnp.where(iota(side, 0) == iota(side, 1), ends_col, 0), 0)
    return keep_row, order, order_rows, keep_col, ends


def kernel(
    n_row, n_col, chunks, group,
    vec_hbm, blk_hbm, ptr_hbm, col_hbm, out_ref,
    vec, blk, ptr_s, col_s, ptr_v, col_v, table_v, table_s,
    row_side, col_side, run, fwd, bwd, near, fwd_in, bwd_in,
    vec_sem, blk_sem, idx_sem,
    rs_send, rs_recv, cs_send, cs_recv, near_send, near_recv,
    f_send, f_recv, b_send, b_recv,
):
    r = lax.axis_index("row")
    c = lax.axis_index("col")
    z, core = c // 2, c % 2
    nz = n_col // 2
    seg = vec.shape[1] // 128
    slots = blk.shape[0]
    per = slots // chunks
    f32 = jnp.float32

    get_vec = pltpu.make_async_copy(vec_hbm, vec, vec_sem)
    get_vec.start()
    barrier = pltpu.get_barrier_semaphore()

    @pl.loop(1, n_row)
    def _(d):
        pl.semaphore_signal(barrier, inc=1, device_id=((r + d) % n_row, c), device_id_type=MESH)

    @pl.loop(1, n_col)
    def _(d):
        pl.semaphore_signal(barrier, inc=1, device_id=(r, (c + d) % n_col), device_id_type=MESH)

    index_copies = [
        pltpu.make_async_copy(src, dst, idx_sem.at[k])
        for k, (src, dst) in enumerate(
            ((ptr_hbm, ptr_v), (col_hbm, col_v), (ptr_hbm, ptr_s), (col_hbm, col_s))
        )
    ]
    for copy in index_copies:
        copy.start()

    def chunk_copy(k):
        part = pl.ds(k * per, per)
        return pltpu.make_async_copy(blk_hbm.at[0, part], blk.at[part], blk_sem.at[k])

    for k in range(chunks):
        chunk_copy(k).start()

    get_vec.wait()
    for u in range(seg):
        piece = vec[:, u * 128:(u + 1) * 128]
        row_side[c * seg + u] = piece
        col_side[r * seg + u] = piece
    pl.semaphore_wait(barrier, n_row + n_col - 2)

    def cs_copy(d, mine):
        owner = r if mine else (r + n_row - d) % n_row
        part = pl.ds(owner * seg, seg)
        return pltpu.make_async_remote_copy(
            src_ref=col_side.at[part], dst_ref=col_side.at[part],
            send_sem=cs_send.at[d], recv_sem=cs_recv.at[d],
            device_id=((r + d) % n_row, c), device_id_type=MESH)

    def rs_copy(d, mine):
        owner = c if mine else (c + n_col - d) % n_col
        part = pl.ds(owner * seg, seg)
        return pltpu.make_async_remote_copy(
            src_ref=row_side.at[part], dst_ref=row_side.at[part],
            send_sem=rs_send.at[d], recv_sem=rs_recv.at[d],
            device_id=(r, (c + d) % n_col), device_id_type=MESH)

    @pl.loop(1, n_row)
    def _(d):
        cs_copy(d, True).start()

    @pl.loop(1, n_col)
    def _(d):
        rs_copy(d, True).start()

    for copy in index_copies:
        copy.wait()
    table_v[...] = jnp.zeros_like(table_v)
    tables = slot_tables(ptr_v[...], col_v[...], n_row * seg)
    for k, entry in enumerate(tables):
        table_v[k:k + 1, 0:entry.shape[1]] = entry
    put_table = pltpu.make_async_copy(table_v, table_s, idx_sem.at[0])
    put_table.start()
    run[slots] = jnp.zeros(run.shape[1:], f32)
    put_table.wait()

    @pl.loop(1, n_row)
    def _(d):
        cs_copy(d, False).wait_recv()

    def four_terms(sides, tiles, across):
        if len(sides) != 4:
            return [
                lax.dot_general(x, t, (((1,), (across,)), ((), ())), preferred_element_type=f32)
                for x, t in zip(sides, tiles)
            ]
        none = jnp.zeros_like(sides[0])
        rows = [[sides[0], none], [sides[1], none], [none, sides[2]], [none, sides[3]]]
        left = jnp.concatenate([jnp.concatenate(pair, 1) for pair in rows], 0)
        places = ((0, 2), (1, 3)) if across else ((0, 1), (2, 3))
        right = jnp.concatenate([jnp.concatenate([tiles[k] for k in pair], 1) for pair in places], 0)
        out = lax.dot_general(left, right, (((1,), (across,)), ((), ())), preferred_element_type=f32)
        m, n = none.shape
        return [out[k * m:(k + 1) * m, (k % 2) * n:(k % 2 + 1) * n] for k in range(4)]

    step = math.gcd(group, 4)

    def group_loop(side_of, tile_of, keep_row, across):
        def one_group(g, total):
            for j in range(0, group, step):
                ids = [g * group + j + k for k in range(step)]
                terms = four_terms([side_of(s) for s in ids], [tile_of(s) for s in ids], across)
                for s, term in zip(ids, terms):
                    total = total * table_s[keep_row, s].astype(f32) + term
                    run[s] = total
            return total
        return one_group

    forward_group = group_loop(lambda s: col_side[col_s[0, s]], lambda s: blk[s], 0, 1)
    backward_group = group_loop(
        lambda s: row_side[table_s[2, s]], lambda s: blk[table_s[1, s]], 3, 0)

    total = jnp.zeros(run.shape[1:], f32)
    for k in range(chunks):
        chunk_copy(k).wait()
        total = lax.fori_loop(k * per // group, (k + 1) * per // group, forward_group, total)

    @pl.loop(0, n_col)
    def _(p):
        for u in range(seg):
            first, last = ptr_s[0, p * seg + u], ptr_s[0, p * seg + u + 1]
            fwd[p % 2, p // 2, u] = run[jnp.where(last > first, last - 1, slots)]

    near_copy = pltpu.make_async_remote_copy(
        src_ref=fwd.at[1 - core], dst_ref=near, send_sem=near_send, recv_sem=near_recv,
        device_id=(r, z * 2 + 1 - core), device_id_type=MESH)
    near_copy.start()

    @pl.loop(1, n_col)
    def _(d):
        rs_copy(d, False).wait_recv()

    def f_copy(d, mine):
        to = (z + d) % nz
        return pltpu.make_async_remote_copy(
            src_ref=fwd.at[core, to], dst_ref=fwd_in.at[z if mine else (z + nz - d) % nz],
            send_sem=f_send.at[d], recv_sem=f_recv.at[d],
            device_id=(r, to * 2 + core), device_id_type=MESH)

    groups = slots // group
    early = max(groups // 4, 1)
    total = lax.fori_loop(0, early, backward_group, jnp.zeros(run.shape[1:], f32))
    near_copy.wait()

    @pl.loop(0, nz)
    def _(p):
        fwd[core, p] = fwd[core, p] + near[p]

    @pl.loop(1, nz)
    def _(d):
        f_copy(d, True).start()

    lax.fori_loop(early, groups, backward_group, total)

    @pl.loop(0, n_row)
    def _(p):
        for u in range(seg):
            q = p * seg + u
            last = table_s[4, q]
            first = jnp.where(q > 0, table_s[4, jnp.maximum(q - 1, 0)], 0)
            bwd[p, u] = run[jnp.where(last > first, last - 1, slots)]

    def b_copy(d, mine):
        to = (r + d) % n_row
        return pltpu.make_async_remote_copy(
            src_ref=bwd.at[to], dst_ref=bwd_in.at[r if mine else (r + n_row - d) % n_row],
            send_sem=b_send.at[d], recv_sem=b_recv.at[d],
            device_id=(to, c), device_id_type=MESH)

    @pl.loop(1, n_row)
    def _(d):
        b_copy(d, True).start()

    bwd_in[r] = bwd[r]
    fwd_in[z] = fwd[core, z]

    @pl.loop(1, nz)
    def _(d):
        f_copy(d, False).wait_recv()

    parts = [fwd_in[p] for p in range(nz)]

    @pl.loop(1, n_row)
    def _(d):
        b_copy(d, False).wait_recv()

    parts = parts + [bwd_in[p] for p in range(n_row)]
    result = functools.reduce(lambda a, b: a + b, parts)
    for u in range(seg):
        out_ref[:, u * 128:(u + 1) * 128] = result[u]

    @pl.loop(1, n_row)
    def _(d):
        cs_copy(d, True).wait_send()
        b_copy(d, True).wait_send()

    @pl.loop(1, n_col)
    def _(d):
        rs_copy(d, True).wait_send()

    @pl.loop(1, nz)
    def _(d):
        f_copy(d, True).wait_send()


def body(n_row, n_col, vectors, blocks, row_ptr, col_idx):
    count, segment = vectors.shape
    slots, edge = blocks.shape[1], blocks.shape[2]
    seg = segment // edge
    group = math.gcd(slots, GROUP)
    chunks = slots // group
    i32, f32, bf16 = jnp.int32, jnp.float32, jnp.bfloat16
    width = -(-max(slots, n_row * seg) // 128) * 128
    nz = n_col // 2
    dma = pltpu.SemaphoreType.DMA
    anywhere = pl.BlockSpec(memory_space=pltpu.HBM)
    return pl.pallas_call(
        functools.partial(kernel, n_row, n_col, chunks, group),
        out_shape=jax.ShapeDtypeStruct((count, segment), f32),
        in_specs=[anywhere] * 4,
        out_specs=pl.BlockSpec(memory_space=pltpu.VMEM),
        scratch_shapes=[
            pltpu.VMEM((count, segment), bf16),
            pltpu.VMEM((slots, edge, edge), bf16),
            pltpu.SMEM(row_ptr.shape, i32),
            pltpu.SMEM(col_idx.shape, i32),
            pltpu.VMEM(row_ptr.shape, i32),
            pltpu.VMEM(col_idx.shape, i32),
            pltpu.VMEM((8, width), i32),
            pltpu.SMEM((8, width), i32),
            pltpu.VMEM((n_col * seg, count, edge), bf16),
            pltpu.VMEM((n_row * seg, count, edge), bf16),
            pltpu.VMEM((slots + 1, count, edge), f32),
            pltpu.VMEM((2, nz, seg, count, edge), f32),
            pltpu.VMEM((n_row, seg, count, edge), f32),
            pltpu.VMEM((nz, seg, count, edge), f32),
            pltpu.VMEM((nz, seg, count, edge), f32),
            pltpu.VMEM((n_row, seg, count, edge), f32),
            dma, dma((chunks,)), dma((4,)),
            dma((n_col,)), dma((n_col,)), dma((n_row,)), dma((n_row,)), dma, dma,
            dma((nz,)), dma((nz,)), dma((n_row,)), dma((n_row,)),
        ],
        compiler_params=pltpu.CompilerParams(
            collective_id=0, has_side_effects=True, vmem_limit_bytes=60 * 1024 * 1024),
        cost_estimate=pl.CostEstimate(
            flops=4 * slots * count * edge * edge, bytes_accessed=2 * slots * edge * edge, transcendentals=0),
    )(vectors, blocks, row_ptr, col_idx)


def solution(mesh):
    in_specs = (
        P(None, ("row", "col")),
        P("row", "col", None, None),
        P("row", "col"),
        P("row", "col"),
    )
    out_specs = P(None, ("row", "col"))
    shape = dict(mesh.shape)
    return jax.shard_map(
        functools.partial(body, shape["row"], shape["col"]),
        mesh=mesh, in_specs=in_specs, out_specs=out_specs, check_vma=False)
```

```python
import functools
import math

import jax
import jax.numpy as jnp
from jax import lax
from jax.experimental import pallas as pl
from jax.experimental.pallas import tpu as pltpu
from jax.sharding import PartitionSpec as P

MESH = pl.DeviceIdType.MESH
GROUP = 48
FAR = 1 << 20


def slot_tables(pointers, columns, tile_cols):
    slots = columns.shape[1]
    tile_rows = pointers.shape[1] - 1
    i32 = jnp.int32

    def iota(shape, dim):
        return lax.broadcasted_iota(i32, shape, dim)

    def total(mask_or_value, axis):
        return jnp.sum(mask_or_value, axis=axis, keepdims=True)

    def count(mask, axis):
        return total(jnp.where(mask, 1, 0), axis)

    corner = (tile_rows + 1, tile_rows + 1)
    pointer_col = total(jnp.where(iota(corner, 0) == iota(corner, 1), pointers, 0), 1)
    wide = (tile_rows + 1, slots)
    rows = count(pointer_col <= iota(wide, 1), 0) - 1
    keep_row = jnp.where(count(pointer_col == iota(wide, 1), 0) == 0, 1, 0)

    square = (slots, slots)
    lane, sub = iota(square, 1), iota(square, 0)
    slot_row = iota((1, slots), 1)
    key = jnp.where(rows < tile_rows, columns * slots, FAR) + slot_row
    rows = jnp.minimum(rows, tile_rows - 1)
    same = lane == sub
    key_col = total(jnp.where(same, key, 0), 1)
    rows_col = total(jnp.where(same, rows, 0), 1)
    rank_col = count(key < key_col, 1)
    chosen = rank_col == lane
    order = total(jnp.where(chosen, sub, 0), 0)
    order_rows = total(jnp.where(chosen, rows_col, 0), 0)
    tall = (tile_cols, slots)
    ends_col = count(key < (iota(tall, 0) + 1) * slots, 1)
    starts = count(ends_col == iota(tall, 1), 0)
    keep_col = jnp.where((starts == 0) & (slot_row > 0), 1, 0)
    side = (tile_cols, tile_cols)
    ends = total(jnp.where(iota(side, 0) == iota(side, 1), ends_col, 0), 0)
    return keep_row, order, order_rows, keep_col, ends


def kernel(
    n_row, n_col, chunks, group,
    vec_hbm, blk_hbm, ptr_hbm, col_hbm, out_ref,
    blk, ptr_s, col_s, ptr_v, col_v, table_v, table_s,
    row_side, col_side, row_blocks, col_blocks, run, fwd, bwd, near, fwd_in, bwd_in,
    here, vec_sem, blk_sem, idx_sem,
    rs_send, rs_recv, cs_send, cs_recv, near_send, near_recv,
    f_send, f_recv, b_send, b_recv,
):
    r = lax.axis_index("row")
    c = lax.axis_index("col")
    z, core = c // 2, c % 2
    nz = n_col // 2
    edge = blk.shape[1]
    seg = vec_hbm.shape[1] // edge
    slots = blk.shape[0]
    per = slots // chunks
    f32 = jnp.float32

    barrier = pltpu.get_barrier_semaphore()

    @pl.loop(1, n_row)
    def _(d):
        pl.semaphore_signal(barrier, inc=1, device_id=((r + d) % n_row, c), device_id_type=MESH)

    @pl.loop(c + 1, n_col)
    def _(p):
        pl.semaphore_signal(barrier, inc=1, device_id=(r, p), device_id_type=MESH)

    own_copies = [
        pltpu.make_async_copy(vec_hbm, dst, vec_sem.at[k])
        for k, dst in enumerate((col_side.at[r], row_side.at[c]))
    ]
    index_copies = [
        pltpu.make_async_copy(src, dst, idx_sem.at[k])
        for k, (src, dst) in enumerate(
            ((ptr_hbm, ptr_v), (col_hbm, col_v), (ptr_hbm, ptr_s), (col_hbm, col_s))
        )
    ]
    for copy in index_copies + own_copies:
        copy.start()

    def chunk_copy(k):
        part = pl.ds(k * per, per)
        return pltpu.make_async_copy(blk_hbm.at[0, part], blk.at[part], blk_sem.at[k])

    for k in range(chunks):
        chunk_copy(k).start()

    pl.semaphore_wait(barrier, n_row - 1 + c)

    def cs_copy(d, mine):
        owner = r if mine else (r + n_row - d) % n_row
        return pltpu.make_async_remote_copy(
            src_ref=vec_hbm, dst_ref=col_side.at[owner],
            send_sem=cs_send.at[d], recv_sem=cs_recv.at[d],
            device_id=((r + d) % n_row, c), device_id_type=MESH)

    def rs_copy(to, source):
        return pltpu.make_async_remote_copy(
            src_ref=vec_hbm, dst_ref=row_side.at[source],
            send_sem=rs_send.at[to], recv_sem=rs_recv.at[source],
            device_id=(r, to), device_id_type=MESH)

    @pl.loop(1, n_row)
    def _(d):
        cs_copy(d, True).start()

    @pl.loop(0, c)
    def _(p):
        pl.semaphore_signal(here, inc=1, device_id=(r, p), device_id_type=MESH)
        rs_copy(p, c).start()

    for copy in index_copies:
        copy.wait()
    table_v[...] = jnp.zeros_like(table_v)
    tables = slot_tables(ptr_v[...], col_v[...], n_row * seg)
    for k, entry in enumerate(tables):
        table_v[k:k + 1, 0:entry.shape[1]] = entry
    put_table = pltpu.make_async_copy(table_v, table_s, idx_sem.at[0])
    put_table.start()
    run[slots] = jnp.zeros(run.shape[1:], f32)
    put_table.wait()

    @pl.loop(1, n_row)
    def _(d):
        cs_copy(d, False).wait_recv()

    for copy in own_copies:
        copy.wait()

    def four_terms(sides, tiles, across):
        if len(sides) != 4:
            return [
                lax.dot_general(x, t, (((1,), (across,)), ((), ())), preferred_element_type=f32)
                for x, t in zip(sides, tiles)
            ]
        none = jnp.zeros_like(sides[0])
        rows = [[sides[0], none], [sides[1], none], [none, sides[2]], [none, sides[3]]]
        left = jnp.concatenate([jnp.concatenate(pair, 1) for pair in rows], 0)
        places = ((0, 2), (1, 3)) if across else ((0, 1), (2, 3))
        right = jnp.concatenate([jnp.concatenate([tiles[k] for k in pair], 1) for pair in places], 0)
        out = lax.dot_general(left, right, (((1,), (across,)), ((), ())), preferred_element_type=f32)
        m, n = none.shape
        return [out[k * m:(k + 1) * m, (k % 2) * n:(k % 2 + 1) * n] for k in range(4)]

    step = math.gcd(group, 4)

    def group_loop(side_of, tile_of, keep_row, across):
        def one_group(g, total):
            for j in range(0, group, step):
                ids = [g * group + j + k for k in range(step)]
                terms = four_terms([side_of(s) for s in ids], [tile_of(s) for s in ids], across)
                for s, term in zip(ids, terms):
                    total = total * table_s[keep_row, s].astype(f32) + term
                    run[s] = total
            return total
        return one_group

    def split(side, out, owners):
        @pl.loop(0, owners)
        def _(p):
            for u in range(seg):
                out[p * seg + u] = side[p, :, u * edge:(u + 1) * edge]

    forward_group = group_loop(lambda s: col_blocks[col_s[0, s]], lambda s: blk[s], 0, 1)
    backward_group = group_loop(
        lambda s: row_blocks[table_s[2, s]], lambda s: blk[table_s[1, s]], 3, 0)

    split(col_side, col_blocks, n_row)
    total = jnp.zeros(run.shape[1:], f32)
    for k in range(chunks):
        chunk_copy(k).wait()
        total = lax.fori_loop(k * per // group, (k + 1) * per // group, forward_group, total)

    @pl.loop(0, n_col)
    def _(p):
        for u in range(seg):
            first, last = ptr_s[0, p * seg + u], ptr_s[0, p * seg + u + 1]
            fwd[p % 2, p // 2, u] = run[jnp.where(last > first, last - 1, slots)]

    @pl.when(c < n_col - 1)
    def _():
        pl.semaphore_wait(here, n_col - 1 - c)

    @pl.loop(c + 1, n_col)
    def _(p):
        rs_copy(p, c).start()

    near_copy = pltpu.make_async_remote_copy(
        src_ref=fwd.at[1 - core], dst_ref=near, send_sem=near_send, recv_sem=near_recv,
        device_id=(r, z * 2 + 1 - core), device_id_type=MESH)
    near_copy.start()

    @pl.loop(1, n_col)
    def _(d):
        p = (c + d) % n_col
        rs_copy(p, p).wait_recv()

    split(row_side, row_blocks, n_col)

    def f_copy(d, mine):
        to = (z + d) % nz
        return pltpu.make_async_remote_copy(
            src_ref=fwd.at[core, to], dst_ref=fwd_in.at[z if mine else (z + nz - d) % nz],
            send_sem=f_send.at[d], recv_sem=f_recv.at[d],
            device_id=(r, to * 2 + core), device_id_type=MESH)

    groups = slots // group
    early = max(groups // 4, 1)
    total = lax.fori_loop(0, early, backward_group, jnp.zeros(run.shape[1:], f32))
    near_copy.wait()

    @pl.loop(0, nz)
    def _(p):
        fwd[core, p] = fwd[core, p] + near[p]

    @pl.loop(1, nz)
    def _(d):
        f_copy(d, True).start()

    lax.fori_loop(early, groups, backward_group, total)

    @pl.loop(0, n_row)
    def _(p):
        for u in range(seg):
            q = p * seg + u
            last = table_s[4, q]
            first = jnp.where(q > 0, table_s[4, jnp.maximum(q - 1, 0)], 0)
            bwd[p, u] = run[jnp.where(last > first, last - 1, slots)]

    def b_copy(d, mine):
        to = (r + d) % n_row
        return pltpu.make_async_remote_copy(
            src_ref=bwd.at[to], dst_ref=bwd_in.at[r if mine else (r + n_row - d) % n_row],
            send_sem=b_send.at[d], recv_sem=b_recv.at[d],
            device_id=(to, c), device_id_type=MESH)

    @pl.loop(1, n_row)
    def _(d):
        b_copy(d, True).start()

    bwd_in[r] = bwd[r]
    fwd_in[z] = fwd[core, z]

    @pl.loop(1, nz)
    def _(d):
        f_copy(d, False).wait_recv()

    parts = [fwd_in[p] for p in range(nz)]

    @pl.loop(1, n_row)
    def _(d):
        b_copy(d, False).wait_recv()

    parts = parts + [bwd_in[p] for p in range(n_row)]
    result = functools.reduce(lambda a, b: a + b, parts)
    for u in range(seg):
        out_ref[:, u * 128:(u + 1) * 128] = result[u]

    @pl.loop(1, n_row)
    def _(d):
        cs_copy(d, True).wait_send()
        b_copy(d, True).wait_send()

    @pl.loop(1, n_col)
    def _(d):
        rs_copy((c + d) % n_col, c).wait_send()

    @pl.loop(1, nz)
    def _(d):
        f_copy(d, True).wait_send()


def body(n_row, n_col, vectors, blocks, row_ptr, col_idx):
    count, segment = vectors.shape
    slots, edge = blocks.shape[1], blocks.shape[2]
    seg = segment // edge
    group = math.gcd(slots, GROUP)
    chunks = slots // group
    i32, f32, bf16 = jnp.int32, jnp.float32, jnp.bfloat16
    width = -(-max(slots, n_row * seg) // 128) * 128
    nz = n_col // 2
    dma = pltpu.SemaphoreType.DMA
    anywhere = pl.BlockSpec(memory_space=pltpu.HBM)
    return pl.pallas_call(
        functools.partial(kernel, n_row, n_col, chunks, group),
        out_shape=jax.ShapeDtypeStruct((count, segment), f32),
        in_specs=[anywhere] * 4,
        out_specs=pl.BlockSpec(memory_space=pltpu.VMEM),
        scratch_shapes=[
            pltpu.VMEM((slots, edge, edge), bf16),
            pltpu.SMEM(row_ptr.shape, i32),
            pltpu.SMEM(col_idx.shape, i32),
            pltpu.VMEM(row_ptr.shape, i32),
            pltpu.VMEM(col_idx.shape, i32),
            pltpu.VMEM((8, width), i32),
            pltpu.SMEM((8, width), i32),
            pltpu.VMEM((n_col, count, segment), bf16),
            pltpu.VMEM((n_row, count, segment), bf16),
            pltpu.VMEM((n_col * seg, count, edge), bf16),
            pltpu.VMEM((n_row * seg, count, edge), bf16),
            pltpu.VMEM((slots + 1, count, edge), f32),
            pltpu.VMEM((2, nz, seg, count, edge), f32),
            pltpu.VMEM((n_row, seg, count, edge), f32),
            pltpu.VMEM((nz, seg, count, edge), f32),
            pltpu.VMEM((nz, seg, count, edge), f32),
            pltpu.VMEM((n_row, seg, count, edge), f32),
            pltpu.SemaphoreType.REGULAR, dma((2,)), dma((chunks,)), dma((4,)),
            dma((n_col,)), dma((n_col,)), dma((n_row,)), dma((n_row,)), dma, dma,
            dma((nz,)), dma((nz,)), dma((n_row,)), dma((n_row,)),
        ],
        compiler_params=pltpu.CompilerParams(
            collective_id=0, has_side_effects=True, vmem_limit_bytes=60 * 1024 * 1024),
        cost_estimate=pl.CostEstimate(
            flops=4 * slots * count * edge * edge, bytes_accessed=2 * slots * edge * edge, transcendentals=0),
    )(vectors, blocks, row_ptr, col_idx)


def solution(mesh):
    in_specs = (
        P(None, ("row", "col")),
        P("row", "col", None, None),
        P("row", "col"),
        P("row", "col"),
    )
    out_specs = P(None, ("row", "col"))
    shape = dict(mesh.shape)
    return jax.shard_map(
        functools.partial(body, shape["row"], shape["col"]),
        mesh=mesh, in_specs=in_specs, out_specs=out_specs, check_vma=False)
```

```python
import functools
import math

import jax
import jax.numpy as jnp
from jax import lax
from jax.experimental import pallas as pl
from jax.experimental.pallas import tpu as pltpu
from jax.sharding import PartitionSpec as P

MESH = pl.DeviceIdType.MESH
GROUP = 48
FAR = 1 << 20


def slot_tables(pointers, columns, tile_cols):
    slots = columns.shape[1]
    tile_rows = pointers.shape[1] - 1
    i32 = jnp.int32

    def iota(shape, dim):
        return lax.broadcasted_iota(i32, shape, dim)

    def total(mask_or_value, axis):
        return jnp.sum(mask_or_value, axis=axis, keepdims=True)

    def count(mask, axis):
        return total(jnp.where(mask, 1, 0), axis)

    corner = (tile_rows + 1, tile_rows + 1)
    pointer_col = total(jnp.where(iota(corner, 0) == iota(corner, 1), pointers, 0), 1)
    wide = (tile_rows + 1, slots)
    rows = count(pointer_col <= iota(wide, 1), 0) - 1
    keep_row = jnp.where(count(pointer_col == iota(wide, 1), 0) == 0, 1, 0)

    square = (slots, slots)
    lane, sub = iota(square, 1), iota(square, 0)
    slot_row = iota((1, slots), 1)
    key = jnp.where(rows < tile_rows, columns * slots, FAR) + slot_row
    rows = jnp.minimum(rows, tile_rows - 1)
    same = lane == sub
    key_col = total(jnp.where(same, key, 0), 1)
    rows_col = total(jnp.where(same, rows, 0), 1)
    rank_col = count(key < key_col, 1)
    chosen = rank_col == lane
    order = total(jnp.where(chosen, sub, 0), 0)
    order_rows = total(jnp.where(chosen, rows_col, 0), 0)
    tall = (tile_cols, slots)
    ends_col = count(key < (iota(tall, 0) + 1) * slots, 1)
    starts = count(ends_col == iota(tall, 1), 0)
    keep_col = jnp.where((starts == 0) & (slot_row > 0), 1, 0)
    side = (tile_cols, tile_cols)
    ends = total(jnp.where(iota(side, 0) == iota(side, 1), ends_col, 0), 0)
    return keep_row, order, order_rows, keep_col, ends


def kernel(
    n_row, n_col, chunks, group,
    vec_hbm, blk_hbm, ptr_hbm, col_hbm, out_ref,
    blk, ptr_s, col_s, ptr_v, col_v, table_v, table_s,
    row_side, col_side, row_blocks, col_blocks, run, fwd, bwd, near, fwd_in, bwd_in,
    here, vec_sem, blk_sem, idx_sem,
    rs_send, rs_recv, cs_send, cs_recv, near_send, near_recv,
    f_send, f_recv, b_send, b_recv,
):
    r = lax.axis_index("row")
    c = lax.axis_index("col")
    z, core = c // 2, c % 2
    nz = n_col // 2
    edge = blk.shape[1]
    seg = vec_hbm.shape[1] // edge
    slots = blk.shape[0]
    per = slots // chunks
    f32 = jnp.float32

    own_copies = [
        pltpu.make_async_copy(vec_hbm, dst, vec_sem.at[k])
        for k, dst in enumerate((col_side.at[r], row_side.at[c]))
    ]
    for copy in own_copies:
        copy.start()

    barrier = pltpu.get_barrier_semaphore()

    @pl.loop(1, n_row)
    def _(d):
        pl.semaphore_signal(barrier, inc=1, device_id=((r + d) % n_row, c), device_id_type=MESH)

    @pl.loop(c + 1, n_col)
    def _(p):
        pl.semaphore_signal(barrier, inc=1, device_id=(r, p), device_id_type=MESH)

    index_copies = [
        pltpu.make_async_copy(src, dst, idx_sem.at[k])
        for k, (src, dst) in enumerate(
            ((ptr_hbm, ptr_v), (col_hbm, col_v), (ptr_hbm, ptr_s), (col_hbm, col_s))
        )
    ]
    for copy in index_copies:
        copy.start()

    def chunk_copy(k):
        part = pl.ds(k * per, per)
        return pltpu.make_async_copy(blk_hbm.at[0, part], blk.at[part], blk_sem.at[k])

    for copy in own_copies:
        copy.wait()
    pl.semaphore_wait(barrier, n_row - 1 + c)

    def cs_copy(d, mine):
        owner = r if mine else (r + n_row - d) % n_row
        return pltpu.make_async_remote_copy(
            src_ref=col_side.at[r], dst_ref=col_side.at[owner],
            send_sem=cs_send.at[d], recv_sem=cs_recv.at[d],
            device_id=((r + d) % n_row, c), device_id_type=MESH)

    def rs_copy(to, source):
        return pltpu.make_async_remote_copy(
            src_ref=row_side.at[c], dst_ref=row_side.at[source],
            send_sem=rs_send.at[to], recv_sem=rs_recv.at[source],
            device_id=(r, to), device_id_type=MESH)

    @pl.loop(1, n_row)
    def _(d):
        cs_copy(d, True).start()

    @pl.loop(0, c)
    def _(p):
        pl.semaphore_signal(here, inc=1, device_id=(r, p), device_id_type=MESH)
        rs_copy(p, c).start()

    for k in range(chunks):
        chunk_copy(k).start()

    for copy in index_copies:
        copy.wait()
    table_v[...] = jnp.zeros_like(table_v)
    tables = slot_tables(ptr_v[...], col_v[...], n_row * seg)
    for k, entry in enumerate(tables):
        table_v[k:k + 1, 0:entry.shape[1]] = entry
    put_table = pltpu.make_async_copy(table_v, table_s, idx_sem.at[0])
    put_table.start()
    run[slots] = jnp.zeros(run.shape[1:], f32)
    put_table.wait()

    @pl.loop(1, n_row)
    def _(d):
        cs_copy(d, False).wait_recv()

    def four_terms(sides, tiles, across):
        if len(sides) != 4:
            return [
                lax.dot_general(x, t, (((1,), (across,)), ((), ())), preferred_element_type=f32)
                for x, t in zip(sides, tiles)
            ]
        none = jnp.zeros_like(sides[0])
        rows = [[sides[0], none], [sides[1], none], [none, sides[2]], [none, sides[3]]]
        left = jnp.concatenate([jnp.concatenate(pair, 1) for pair in rows], 0)
        places = ((0, 2), (1, 3)) if across else ((0, 1), (2, 3))
        right = jnp.concatenate([jnp.concatenate([tiles[k] for k in pair], 1) for pair in places], 0)
        out = lax.dot_general(left, right, (((1,), (across,)), ((), ())), preferred_element_type=f32)
        m, n = none.shape
        return [out[k * m:(k + 1) * m, (k % 2) * n:(k % 2 + 1) * n] for k in range(4)]

    step = math.gcd(group, 4)

    def group_loop(side_of, tile_of, keep_row, across):
        def one_group(g, total):
            for j in range(0, group, step):
                ids = [g * group + j + k for k in range(step)]
                terms = four_terms([side_of(s) for s in ids], [tile_of(s) for s in ids], across)
                for s, term in zip(ids, terms):
                    total = total * table_s[keep_row, s].astype(f32) + term
                    run[s] = total
            return total
        return one_group

    def split(side, out, owners):
        @pl.loop(0, owners)
        def _(p):
            for u in range(seg):
                out[p * seg + u] = side[p, :, u * edge:(u + 1) * edge]

    forward_group = group_loop(lambda s: col_blocks[col_s[0, s]], lambda s: blk[s], 0, 1)
    backward_group = group_loop(
        lambda s: row_blocks[table_s[2, s]], lambda s: blk[table_s[1, s]], 3, 0)

    split(col_side, col_blocks, n_row)
    total = jnp.zeros(run.shape[1:], f32)
    for k in range(chunks):
        chunk_copy(k).wait()
        total = lax.fori_loop(k * per // group, (k + 1) * per // group, forward_group, total)
        if k == (chunks - 1) // 2:
            @pl.when(c < n_col - 1)
            def _():
                pl.semaphore_wait(here, n_col - 1 - c)

            @pl.loop(c + 1, n_col)
            def _(p):
                rs_copy(p, c).start()

    @pl.loop(0, n_col)
    def _(p):
        for u in range(seg):
            first, last = ptr_s[0, p * seg + u], ptr_s[0, p * seg + u + 1]
            fwd[p % 2, p // 2, u] = run[jnp.where(last > first, last - 1, slots)]

    near_copy = pltpu.make_async_remote_copy(
        src_ref=fwd.at[1 - core], dst_ref=near, send_sem=near_send, recv_sem=near_recv,
        device_id=(r, z * 2 + 1 - core), device_id_type=MESH)
    near_copy.start()

    @pl.loop(1, n_col)
    def _(d):
        p = (c + d) % n_col
        rs_copy(p, p).wait_recv()

    split(row_side, row_blocks, n_col)

    def f_copy(d, mine):
        to = (z + d) % nz
        return pltpu.make_async_remote_copy(
            src_ref=fwd.at[core, to], dst_ref=fwd_in.at[z if mine else (z + nz - d) % nz],
            send_sem=f_send.at[d], recv_sem=f_recv.at[d],
            device_id=(r, to * 2 + core), device_id_type=MESH)

    groups = slots // group
    early = max(groups // 4, 1)
    total = lax.fori_loop(0, early, backward_group, jnp.zeros(run.shape[1:], f32))
    near_copy.wait()

    @pl.loop(0, nz)
    def _(p):
        fwd[core, p] = fwd[core, p] + near[p]

    @pl.loop(1, nz)
    def _(d):
        f_copy(d, True).start()

    lax.fori_loop(early, groups, backward_group, total)

    @pl.loop(0, n_row)
    def _(p):
        for u in range(seg):
            q = p * seg + u
            last = table_s[4, q]
            first = jnp.where(q > 0, table_s[4, jnp.maximum(q - 1, 0)], 0)
            bwd[p, u] = run[jnp.where(last > first, last - 1, slots)]

    def b_copy(d, mine):
        to = (r + d) % n_row
        return pltpu.make_async_remote_copy(
            src_ref=bwd.at[to], dst_ref=bwd_in.at[r if mine else (r + n_row - d) % n_row],
            send_sem=b_send.at[d], recv_sem=b_recv.at[d],
            device_id=(to, c), device_id_type=MESH)

    @pl.loop(1, n_row)
    def _(d):
        b_copy(d, True).start()

    bwd_in[r] = bwd[r]
    fwd_in[z] = fwd[core, z]

    @pl.loop(1, nz)
    def _(d):
        f_copy(d, False).wait_recv()

    parts = [fwd_in[p] for p in range(nz)]

    @pl.loop(1, n_row)
    def _(d):
        b_copy(d, False).wait_recv()

    parts = parts + [bwd_in[p] for p in range(n_row)]
    result = functools.reduce(lambda a, b: a + b, parts)
    for u in range(seg):
        out_ref[:, u * 128:(u + 1) * 128] = result[u]

    @pl.loop(1, n_row)
    def _(d):
        cs_copy(d, True).wait_send()
        b_copy(d, True).wait_send()

    @pl.loop(1, n_col)
    def _(d):
        rs_copy((c + d) % n_col, c).wait_send()

    @pl.loop(1, nz)
    def _(d):
        f_copy(d, True).wait_send()


def body(n_row, n_col, vectors, blocks, row_ptr, col_idx):
    count, segment = vectors.shape
    slots, edge = blocks.shape[1], blocks.shape[2]
    seg = segment // edge
    group = math.gcd(slots, GROUP)
    chunks = slots // group
    i32, f32, bf16 = jnp.int32, jnp.float32, jnp.bfloat16
    width = -(-max(slots, n_row * seg) // 128) * 128
    nz = n_col // 2
    dma = pltpu.SemaphoreType.DMA
    anywhere = pl.BlockSpec(memory_space=pltpu.HBM)
    return pl.pallas_call(
        functools.partial(kernel, n_row, n_col, chunks, group),
        out_shape=jax.ShapeDtypeStruct((count, segment), f32),
        in_specs=[anywhere] * 4,
        out_specs=pl.BlockSpec(memory_space=pltpu.VMEM),
        scratch_shapes=[
            pltpu.VMEM((slots, edge, edge), bf16),
            pltpu.SMEM(row_ptr.shape, i32),
            pltpu.SMEM(col_idx.shape, i32),
            pltpu.VMEM(row_ptr.shape, i32),
            pltpu.VMEM(col_idx.shape, i32),
            pltpu.VMEM((8, width), i32),
            pltpu.SMEM((8, width), i32),
            pltpu.VMEM((n_col, count, segment), bf16),
            pltpu.VMEM((n_row, count, segment), bf16),
            pltpu.VMEM((n_col * seg, count, edge), bf16),
            pltpu.VMEM((n_row * seg, count, edge), bf16),
            pltpu.VMEM((slots + 1, count, edge), f32),
            pltpu.VMEM((2, nz, seg, count, edge), f32),
            pltpu.VMEM((n_row, seg, count, edge), f32),
            pltpu.VMEM((nz, seg, count, edge), f32),
            pltpu.VMEM((nz, seg, count, edge), f32),
            pltpu.VMEM((n_row, seg, count, edge), f32),
            pltpu.SemaphoreType.REGULAR, dma((2,)), dma((chunks,)), dma((4,)),
            dma((n_col,)), dma((n_col,)), dma((n_row,)), dma((n_row,)), dma, dma,
            dma((nz,)), dma((nz,)), dma((n_row,)), dma((n_row,)),
        ],
        compiler_params=pltpu.CompilerParams(
            collective_id=0, has_side_effects=True, vmem_limit_bytes=60 * 1024 * 1024),
        cost_estimate=pl.CostEstimate(
            flops=4 * slots * count * edge * edge, bytes_accessed=2 * slots * edge * edge, transcendentals=0),
    )(vectors, blocks, row_ptr, col_idx)


def solution(mesh):
    in_specs = (
        P(None, ("row", "col")),
        P("row", "col", None, None),
        P("row", "col"),
        P("row", "col"),
    )
    out_specs = P(None, ("row", "col"))
    shape = dict(mesh.shape)
    return jax.shard_map(
        functools.partial(body, shape["row"], shape["col"]),
        mesh=mesh, in_specs=in_specs, out_specs=out_specs, check_vma=False)
```

```python
import functools
import math

import jax
import jax.numpy as jnp
from jax import lax
from jax.experimental import pallas as pl
from jax.experimental.pallas import tpu as pltpu
from jax.sharding import PartitionSpec as P

MESH = pl.DeviceIdType.MESH
GROUP = 24
FAR = 1 << 20


def slot_tables(pointers, columns, tile_cols):
    slots = columns.shape[1]
    tile_rows = pointers.shape[1] - 1
    i32 = jnp.int32

    def iota(shape, dim):
        return lax.broadcasted_iota(i32, shape, dim)

    def total(mask_or_value, axis):
        return jnp.sum(mask_or_value, axis=axis, keepdims=True)

    def count(mask, axis):
        return total(jnp.where(mask, 1, 0), axis)

    corner = (tile_rows + 1, tile_rows + 1)
    pointer_col = total(jnp.where(iota(corner, 0) == iota(corner, 1), pointers, 0), 1)
    wide = (tile_rows + 1, slots)
    rows = count(pointer_col <= iota(wide, 1), 0) - 1
    keep_row = jnp.where(count(pointer_col == iota(wide, 1), 0) == 0, 1, 0)

    square = (slots, slots)
    lane, sub = iota(square, 1), iota(square, 0)
    slot_row = iota((1, slots), 1)
    key = jnp.where(rows < tile_rows, columns * slots, FAR) + slot_row
    rows = jnp.minimum(rows, tile_rows - 1)
    same = lane == sub
    key_col = total(jnp.where(same, key, 0), 1)
    rows_col = total(jnp.where(same, rows, 0), 1)
    rank_col = count(key < key_col, 1)
    chosen = rank_col == lane
    order = total(jnp.where(chosen, sub, 0), 0)
    order_rows = total(jnp.where(chosen, rows_col, 0), 0)
    tall = (tile_cols, slots)
    ends_col = count(key < (iota(tall, 0) + 1) * slots, 1)
    starts = count(ends_col == iota(tall, 1), 0)
    keep_col = jnp.where((starts == 0) & (slot_row > 0), 1, 0)
    side = (tile_cols, tile_cols)
    ends = total(jnp.where(iota(side, 0) == iota(side, 1), ends_col, 0), 0)
    return keep_row, order, order_rows, keep_col, ends


def kernel(
    n_row, n_col, chunks, group,
    vec_hbm, blk_hbm, ptr_hbm, col_hbm, out_ref,
    blk, ptr_s, col_s, ptr_v, col_v, table_v, table_s,
    row_side, col_side, row_blocks, col_blocks, run, fwd, bwd, near, fwd_in, bwd_in,
    here, vec_sem, blk_sem, idx_sem,
    rs_send, rs_recv, cs_send, cs_recv, near_send, near_recv,
    f_send, f_recv, b_send, b_recv,
):
    r = lax.axis_index("row")
    c = lax.axis_index("col")
    z, core = c // 2, c % 2
    nz = n_col // 2
    edge = blk.shape[1]
    seg = vec_hbm.shape[1] // edge
    slots = blk.shape[0]
    per = slots // chunks
    f32 = jnp.float32

    own_copies = [
        pltpu.make_async_copy(vec_hbm, dst, vec_sem.at[k])
        for k, dst in enumerate((col_side.at[r], row_side.at[c]))
    ]
    for copy in own_copies:
        copy.start()

    barrier = pltpu.get_barrier_semaphore()

    @pl.loop(1, n_row)
    def _(d):
        pl.semaphore_signal(barrier, inc=1, device_id=((r + d) % n_row, c), device_id_type=MESH)

    @pl.loop(c + 1, n_col)
    def _(p):
        pl.semaphore_signal(barrier, inc=1, device_id=(r, p), device_id_type=MESH)

    index_copies = [
        pltpu.make_async_copy(src, dst, idx_sem.at[k])
        for k, (src, dst) in enumerate(
            ((ptr_hbm, ptr_v), (col_hbm, col_v), (ptr_hbm, ptr_s), (col_hbm, col_s))
        )
    ]
    for copy in index_copies:
        copy.start()

    def chunk_copy(k):
        part = pl.ds(k * per, per)
        return pltpu.make_async_copy(blk_hbm.at[0, part], blk.at[part], blk_sem.at[k])

    for copy in own_copies:
        copy.wait()
    pl.semaphore_wait(barrier, n_row - 1 + c)

    def cs_copy(d, mine):
        owner = r if mine else (r + n_row - d) % n_row
        return pltpu.make_async_remote_copy(
            src_ref=col_side.at[r], dst_ref=col_side.at[owner],
            send_sem=cs_send.at[d], recv_sem=cs_recv.at[d],
            device_id=((r + d) % n_row, c), device_id_type=MESH)

    def rs_copy(to, source):
        return pltpu.make_async_remote_copy(
            src_ref=row_side.at[c], dst_ref=row_side.at[source],
            send_sem=rs_send.at[to], recv_sem=rs_recv.at[source],
            device_id=(r, to), device_id_type=MESH)

    @pl.loop(1, n_row)
    def _(d):
        cs_copy(d, True).start()

    @pl.loop(0, c)
    def _(p):
        pl.semaphore_signal(here, inc=1, device_id=(r, p), device_id_type=MESH)
        rs_copy(p, c).start()

    for k in range(chunks):
        chunk_copy(k).start()

    for copy in index_copies:
        copy.wait()
    table_v[...] = jnp.zeros_like(table_v)
    tables = slot_tables(ptr_v[...], col_v[...], n_row * seg)
    for k, entry in enumerate(tables):
        table_v[k:k + 1, 0:entry.shape[1]] = entry
    put_table = pltpu.make_async_copy(table_v, table_s, idx_sem.at[0])
    put_table.start()
    run[slots] = jnp.zeros(run.shape[1:], f32)
    put_table.wait()

    @pl.loop(1, n_row)
    def _(d):
        cs_copy(d, False).wait_recv()

    def four_terms(sides, tiles, across):
        if len(sides) != 4:
            return [
                lax.dot_general(x, t, (((1,), (across,)), ((), ())), preferred_element_type=f32)
                for x, t in zip(sides, tiles)
            ]
        none = jnp.zeros_like(sides[0])
        rows = [[sides[0], none], [sides[1], none], [none, sides[2]], [none, sides[3]]]
        left = jnp.concatenate([jnp.concatenate(pair, 1) for pair in rows], 0)
        places = ((0, 2), (1, 3)) if across else ((0, 1), (2, 3))
        right = jnp.concatenate([jnp.concatenate([tiles[k] for k in pair], 1) for pair in places], 0)
        out = lax.dot_general(left, right, (((1,), (across,)), ((), ())), preferred_element_type=f32)
        m, n = none.shape
        return [out[k * m:(k + 1) * m, (k % 2) * n:(k % 2 + 1) * n] for k in range(4)]

    step = math.gcd(group, 4)

    def group_loop(side_of, tile_of, keep_row, across):
        def one_group(g, total):
            for j in range(0, group, step):
                ids = [g * group + j + k for k in range(step)]
                terms = four_terms([side_of(s) for s in ids], [tile_of(s) for s in ids], across)
                for s, term in zip(ids, terms):
                    total = total * table_s[keep_row, s].astype(f32) + term
                    run[s] = total
            return total
        return one_group

    def split(side, out, owners):
        @pl.loop(0, owners)
        def _(p):
            for u in range(seg):
                out[p * seg + u] = side[p, :, u * edge:(u + 1) * edge]

    forward_group = group_loop(lambda s: col_blocks[col_s[0, s]], lambda s: blk[s], 0, 1)
    backward_group = group_loop(
        lambda s: row_blocks[table_s[2, s]], lambda s: blk[table_s[1, s]], 3, 0)

    split(col_side, col_blocks, n_row)

    def forward_step(g, total):
        @pl.when(g == chunks // 2)
        def _():
            @pl.when(c < n_col - 1)
            def _():
                pl.semaphore_wait(here, n_col - 1 - c)

            @pl.loop(c + 1, n_col)
            def _(p):
                rs_copy(p, c).start()

        chunk_copy(g).wait()
        return forward_group(g, total)

    lax.fori_loop(0, chunks, forward_step, jnp.zeros(run.shape[1:], f32))

    @pl.loop(0, n_col)
    def _(p):
        for u in range(seg):
            first, last = ptr_s[0, p * seg + u], ptr_s[0, p * seg + u + 1]
            fwd[p % 2, p // 2, u] = run[jnp.where(last > first, last - 1, slots)]

    near_copy = pltpu.make_async_remote_copy(
        src_ref=fwd.at[1 - core], dst_ref=near, send_sem=near_send, recv_sem=near_recv,
        device_id=(r, z * 2 + 1 - core), device_id_type=MESH)
    near_copy.start()

    @pl.loop(1, n_col)
    def _(d):
        p = (c + d) % n_col
        rs_copy(p, p).wait_recv()

    split(row_side, row_blocks, n_col)

    def f_copy(d, mine):
        to = (z + d) % nz
        return pltpu.make_async_remote_copy(
            src_ref=fwd.at[core, to], dst_ref=fwd_in.at[z if mine else (z + nz - d) % nz],
            send_sem=f_send.at[d], recv_sem=f_recv.at[d],
            device_id=(r, to * 2 + core), device_id_type=MESH)

    def backward_step(g, total):
        @pl.when(g == chunks // 4)
        def _():
            near_copy.wait()

            @pl.loop(0, nz)
            def _(p):
                fwd[core, p] = fwd[core, p] + near[p]

            @pl.loop(1, nz)
            def _(d):
                f_copy(d, True).start()

        return backward_group(g, total)

    lax.fori_loop(0, chunks, backward_step, jnp.zeros(run.shape[1:], f32))

    @pl.loop(0, n_row)
    def _(p):
        for u in range(seg):
            q = p * seg + u
            last = table_s[4, q]
            first = jnp.where(q > 0, table_s[4, jnp.maximum(q - 1, 0)], 0)
            bwd[p, u] = run[jnp.where(last > first, last - 1, slots)]

    def b_copy(d, mine):
        to = (r + d) % n_row
        return pltpu.make_async_remote_copy(
            src_ref=bwd.at[to], dst_ref=bwd_in.at[r if mine else (r + n_row - d) % n_row],
            send_sem=b_send.at[d], recv_sem=b_recv.at[d],
            device_id=(to, c), device_id_type=MESH)

    @pl.loop(1, n_row)
    def _(d):
        b_copy(d, True).start()

    bwd_in[r] = bwd[r]
    fwd_in[z] = fwd[core, z]

    @pl.loop(1, nz)
    def _(d):
        f_copy(d, False).wait_recv()

    parts = [fwd_in[p] for p in range(nz)]

    @pl.loop(1, n_row)
    def _(d):
        b_copy(d, False).wait_recv()

    parts = parts + [bwd_in[p] for p in range(n_row)]
    result = functools.reduce(lambda a, b: a + b, parts)
    for u in range(seg):
        out_ref[:, u * 128:(u + 1) * 128] = result[u]

    @pl.loop(1, n_row)
    def _(d):
        cs_copy(d, True).wait_send()
        b_copy(d, True).wait_send()

    @pl.loop(1, n_col)
    def _(d):
        rs_copy((c + d) % n_col, c).wait_send()

    @pl.loop(1, nz)
    def _(d):
        f_copy(d, True).wait_send()


def body(n_row, n_col, vectors, blocks, row_ptr, col_idx):
    count, segment = vectors.shape
    slots, edge = blocks.shape[1], blocks.shape[2]
    seg = segment // edge
    group = math.gcd(slots, GROUP)
    chunks = slots // group
    i32, f32, bf16 = jnp.int32, jnp.float32, jnp.bfloat16
    width = -(-max(slots, n_row * seg) // 128) * 128
    nz = n_col // 2
    dma = pltpu.SemaphoreType.DMA
    anywhere = pl.BlockSpec(memory_space=pltpu.HBM)
    return pl.pallas_call(
        functools.partial(kernel, n_row, n_col, chunks, group),
        out_shape=jax.ShapeDtypeStruct((count, segment), f32),
        in_specs=[anywhere] * 4,
        out_specs=pl.BlockSpec(memory_space=pltpu.VMEM),
        scratch_shapes=[
            pltpu.VMEM((slots, edge, edge), bf16),
            pltpu.SMEM(row_ptr.shape, i32),
            pltpu.SMEM(col_idx.shape, i32),
            pltpu.VMEM(row_ptr.shape, i32),
            pltpu.VMEM(col_idx.shape, i32),
            pltpu.VMEM((8, width), i32),
            pltpu.SMEM((8, width), i32),
            pltpu.VMEM((n_col, count, segment), bf16),
            pltpu.VMEM((n_row, count, segment), bf16),
            pltpu.VMEM((n_col * seg, count, edge), bf16),
            pltpu.VMEM((n_row * seg, count, edge), bf16),
            pltpu.VMEM((slots + 1, count, edge), f32),
            pltpu.VMEM((2, nz, seg, count, edge), f32),
            pltpu.VMEM((n_row, seg, count, edge), f32),
            pltpu.VMEM((nz, seg, count, edge), f32),
            pltpu.VMEM((nz, seg, count, edge), f32),
            pltpu.VMEM((n_row, seg, count, edge), f32),
            pltpu.SemaphoreType.REGULAR, dma((2,)), dma((chunks,)), dma((4,)),
            dma((n_col,)), dma((n_col,)), dma((n_row,)), dma((n_row,)), dma, dma,
            dma((nz,)), dma((nz,)), dma((n_row,)), dma((n_row,)),
        ],
        compiler_params=pltpu.CompilerParams(
            collective_id=0, has_side_effects=True, vmem_limit_bytes=60 * 1024 * 1024),
        cost_estimate=pl.CostEstimate(
            flops=4 * slots * count * edge * edge, bytes_accessed=2 * slots * edge * edge, transcendentals=0),
    )(vectors, blocks, row_ptr, col_idx)


def solution(mesh):
    in_specs = (
        P(None, ("row", "col")),
        P("row", "col", None, None),
        P("row", "col"),
        P("row", "col"),
    )
    out_specs = P(None, ("row", "col"))
    shape = dict(mesh.shape)
    return jax.shard_map(
        functools.partial(body, shape["row"], shape["col"]),
        mesh=mesh, in_specs=in_specs, out_specs=out_specs, check_vma=False)
```

```python
import functools
import math

import jax
import jax.numpy as jnp
from jax import lax
from jax.experimental import pallas as pl
from jax.experimental.pallas import tpu as pltpu
from jax.sharding import PartitionSpec as P

MESH = pl.DeviceIdType.MESH
GROUP = 48
FAR = 1 << 20


def slot_tables(pointers, columns, tile_cols):
    slots = columns.shape[1]
    tile_rows = pointers.shape[1] - 1
    i32 = jnp.int32

    def iota(shape, dim):
        return lax.broadcasted_iota(i32, shape, dim)

    def total(mask_or_value, axis):
        return jnp.sum(mask_or_value, axis=axis, keepdims=True)

    def count(mask, axis):
        return total(jnp.where(mask, 1, 0), axis)

    corner = (tile_rows + 1, tile_rows + 1)
    pointer_col = total(jnp.where(iota(corner, 0) == iota(corner, 1), pointers, 0), 1)
    wide = (tile_rows + 1, slots)
    rows = count(pointer_col <= iota(wide, 1), 0) - 1
    keep_row = jnp.where(count(pointer_col == iota(wide, 1), 0) == 0, 1, 0)

    square = (slots, slots)
    lane, sub = iota(square, 1), iota(square, 0)
    slot_row = iota((1, slots), 1)
    key = jnp.where(rows < tile_rows, columns * slots, FAR) + slot_row
    rows = jnp.minimum(rows, tile_rows - 1)
    same = lane == sub
    key_col = total(jnp.where(same, key, 0), 1)
    rows_col = total(jnp.where(same, rows, 0), 1)
    rank_col = count(key < key_col, 1)
    chosen = rank_col == lane
    order = total(jnp.where(chosen, sub, 0), 0)
    order_rows = total(jnp.where(chosen, rows_col, 0), 0)
    tall = (tile_cols, slots)
    ends_col = count(key < (iota(tall, 0) + 1) * slots, 1)
    starts = count(ends_col == iota(tall, 1), 0)
    keep_col = jnp.where((starts == 0) & (slot_row > 0), 1, 0)
    side = (tile_cols, tile_cols)
    ends = total(jnp.where(iota(side, 0) == iota(side, 1), ends_col, 0), 0)
    return keep_row, order, order_rows, keep_col, ends


def kernel(
    n_row, n_col, chunks, group,
    vec_hbm, blk_hbm, ptr_hbm, col_hbm, out_ref,
    blk, ptr_s, col_s, ptr_v, col_v, table_v, table_s,
    row_side, col_side, row_blocks, col_blocks, run, fwd, bwd, near, fwd_in, bwd_in,
    here, vec_sem, blk_sem, idx_sem,
    rs_send, rs_recv, cs_send, cs_recv, near_send, near_recv,
    f_send, f_recv, b_send, b_recv,
):
    r = lax.axis_index("row")
    c = lax.axis_index("col")
    z, core = c // 2, c % 2
    nz = n_col // 2
    edge = blk.shape[1]
    seg = vec_hbm.shape[1] // edge
    slots = blk.shape[0]
    per = slots // chunks
    f32 = jnp.float32

    own_copies = [
        pltpu.make_async_copy(vec_hbm, dst, vec_sem.at[k])
        for k, dst in enumerate((col_side.at[r], row_side.at[c]))
    ]
    for copy in own_copies:
        copy.start()

    barrier = pltpu.get_barrier_semaphore()

    @pl.loop(1, n_row)
    def _(d):
        pl.semaphore_signal(barrier, inc=1, device_id=((r + d) % n_row, c), device_id_type=MESH)

    @pl.loop(c + 1, n_col)
    def _(p):
        pl.semaphore_signal(barrier, inc=1, device_id=(r, p), device_id_type=MESH)

    index_copies = [
        pltpu.make_async_copy(src, dst, idx_sem.at[k])
        for k, (src, dst) in enumerate(
            ((ptr_hbm, ptr_v), (col_hbm, col_v), (ptr_hbm, ptr_s), (col_hbm, col_s))
        )
    ]
    for copy in index_copies:
        copy.start()

    def chunk_copy(k):
        part = pl.ds(k * per, per)
        return pltpu.make_async_copy(blk_hbm.at[0, part], blk.at[part], blk_sem.at[k])

    for copy in own_copies:
        copy.wait()
    pl.semaphore_wait(barrier, n_row - 1 + c)

    def cs_copy(d, mine):
        owner = r if mine else (r + n_row - d) % n_row
        return pltpu.make_async_remote_copy(
            src_ref=col_side.at[r], dst_ref=col_side.at[owner],
            send_sem=cs_send.at[d], recv_sem=cs_recv.at[d],
            device_id=((r + d) % n_row, c), device_id_type=MESH)

    def rs_copy(to, source):
        return pltpu.make_async_remote_copy(
            src_ref=row_side.at[c], dst_ref=row_side.at[source],
            send_sem=rs_send.at[to], recv_sem=rs_recv.at[source],
            device_id=(r, to), device_id_type=MESH)

    @pl.loop(1, n_row)
    def _(d):
        cs_copy(d, True).start()

    @pl.loop(0, c)
    def _(p):
        pl.semaphore_signal(here, inc=1, device_id=(r, p), device_id_type=MESH)
        rs_copy(p, c).start()

    for k in range(chunks):
        chunk_copy(k).start()

    for copy in index_copies:
        copy.wait()
    table_v[...] = jnp.zeros_like(table_v)
    tables = slot_tables(ptr_v[...], col_v[...], n_row * seg)
    for k, entry in enumerate(tables):
        table_v[k:k + 1, 0:entry.shape[1]] = entry
    put_table = pltpu.make_async_copy(table_v, table_s, idx_sem.at[0])
    put_table.start()
    run[slots] = jnp.zeros(run.shape[1:], f32)
    put_table.wait()

    @pl.loop(1, n_row)
    def _(d):
        cs_copy(d, False).wait_recv()

    def side_by_side(sides, tiles, across):
        left = jnp.concatenate(sides, 0)
        right = jnp.concatenate(tiles, 1 - across)
        out = lax.dot_general(left, right, (((1,), (across,)), ((), ())), preferred_element_type=f32)
        m, n = sides[0].shape
        return [out[k * m:(k + 1) * m, k * n:(k + 1) * n] for k in range(len(sides))]

    step = math.gcd(group, 2)

    def group_loop(side_of, tile_of, keep_row, across):
        def one_group(g, total):
            for j in range(0, group, step):
                ids = [g * group + j + k for k in range(step)]
                terms = side_by_side([side_of(s) for s in ids], [tile_of(s) for s in ids], across)
                for s, term in zip(ids, terms):
                    total = total * table_s[keep_row, s].astype(f32) + term
                    run[s] = total
            return total
        return one_group

    def split(side, out, owners):
        @pl.loop(0, owners)
        def _(p):
            for u in range(seg):
                out[p * seg + u] = side[p, :, u * edge:(u + 1) * edge]

    forward_group = group_loop(lambda s: col_blocks[col_s[0, s]], lambda s: blk[s], 0, 1)
    backward_group = group_loop(
        lambda s: row_blocks[table_s[2, s]], lambda s: blk[table_s[1, s]], 3, 0)

    split(col_side, col_blocks, n_row)

    def forward_step(g, total):
        @pl.when(g == chunks // 2)
        def _():
            @pl.when(c < n_col - 1)
            def _():
                pl.semaphore_wait(here, n_col - 1 - c)

            @pl.loop(c + 1, n_col)
            def _(p):
                rs_copy(p, c).start()

        chunk_copy(g).wait()
        return forward_group(g, total)

    lax.fori_loop(0, chunks, forward_step, jnp.zeros(run.shape[1:], f32))

    @pl.loop(0, n_col)
    def _(p):
        for u in range(seg):
            first, last = ptr_s[0, p * seg + u], ptr_s[0, p * seg + u + 1]
            fwd[p % 2, p // 2, u] = run[jnp.where(last > first, last - 1, slots)]

    near_copy = pltpu.make_async_remote_copy(
        src_ref=fwd.at[1 - core], dst_ref=near, send_sem=near_send, recv_sem=near_recv,
        device_id=(r, z * 2 + 1 - core), device_id_type=MESH)
    near_copy.start()

    @pl.loop(1, n_col)
    def _(d):
        p = (c + d) % n_col
        rs_copy(p, p).wait_recv()

    split(row_side, row_blocks, n_col)

    def f_copy(d, mine):
        to = (z + d) % nz
        return pltpu.make_async_remote_copy(
            src_ref=fwd.at[core, to], dst_ref=fwd_in.at[z if mine else (z + nz - d) % nz],
            send_sem=f_send.at[d], recv_sem=f_recv.at[d],
            device_id=(r, to * 2 + core), device_id_type=MESH)

    def backward_step(g, total):
        @pl.when(g == max(chunks // 4, 1))
        def _():
            near_copy.wait()

            @pl.loop(0, nz)
            def _(p):
                fwd[core, p] = fwd[core, p] + near[p]

            @pl.loop(1, nz)
            def _(d):
                f_copy(d, True).start()

        return backward_group(g, total)

    lax.fori_loop(0, chunks, backward_step, jnp.zeros(run.shape[1:], f32))

    @pl.loop(0, n_row)
    def _(p):
        for u in range(seg):
            q = p * seg + u
            last = table_s[4, q]
            first = jnp.where(q > 0, table_s[4, jnp.maximum(q - 1, 0)], 0)
            bwd[p, u] = run[jnp.where(last > first, last - 1, slots)]

    def b_copy(d, mine):
        to = (r + d) % n_row
        return pltpu.make_async_remote_copy(
            src_ref=bwd.at[to], dst_ref=bwd_in.at[r if mine else (r + n_row - d) % n_row],
            send_sem=b_send.at[d], recv_sem=b_recv.at[d],
            device_id=(to, c), device_id_type=MESH)

    @pl.loop(1, n_row)
    def _(d):
        b_copy(d, True).start()

    bwd_in[r] = bwd[r]
    fwd_in[z] = fwd[core, z]

    @pl.loop(1, nz)
    def _(d):
        f_copy(d, False).wait_recv()

    parts = [fwd_in[p] for p in range(nz)]

    @pl.loop(1, n_row)
    def _(d):
        b_copy(d, False).wait_recv()

    parts = parts + [bwd_in[p] for p in range(n_row)]
    result = functools.reduce(lambda a, b: a + b, parts)
    for u in range(seg):
        out_ref[:, u * 128:(u + 1) * 128] = result[u]

    @pl.loop(1, n_row)
    def _(d):
        cs_copy(d, True).wait_send()
        b_copy(d, True).wait_send()

    @pl.loop(1, n_col)
    def _(d):
        rs_copy((c + d) % n_col, c).wait_send()

    @pl.loop(1, nz)
    def _(d):
        f_copy(d, True).wait_send()


def body(n_row, n_col, vectors, blocks, row_ptr, col_idx):
    count, segment = vectors.shape
    slots, edge = blocks.shape[1], blocks.shape[2]
    seg = segment // edge
    group = math.gcd(slots, GROUP)
    chunks = slots // group
    i32, f32, bf16 = jnp.int32, jnp.float32, jnp.bfloat16
    width = -(-max(slots, n_row * seg) // 128) * 128
    nz = n_col // 2
    dma = pltpu.SemaphoreType.DMA
    anywhere = pl.BlockSpec(memory_space=pltpu.HBM)
    return pl.pallas_call(
        functools.partial(kernel, n_row, n_col, chunks, group),
        out_shape=jax.ShapeDtypeStruct((count, segment), f32),
        in_specs=[anywhere] * 4,
        out_specs=pl.BlockSpec(memory_space=pltpu.VMEM),
        scratch_shapes=[
            pltpu.VMEM((slots, edge, edge), bf16),
            pltpu.SMEM(row_ptr.shape, i32),
            pltpu.SMEM(col_idx.shape, i32),
            pltpu.VMEM(row_ptr.shape, i32),
            pltpu.VMEM(col_idx.shape, i32),
            pltpu.VMEM((8, width), i32),
            pltpu.SMEM((8, width), i32),
            pltpu.VMEM((n_col, count, segment), bf16),
            pltpu.VMEM((n_row, count, segment), bf16),
            pltpu.VMEM((n_col * seg, count, edge), bf16),
            pltpu.VMEM((n_row * seg, count, edge), bf16),
            pltpu.VMEM((slots + 1, count, edge), f32),
            pltpu.VMEM((2, nz, seg, count, edge), f32),
            pltpu.VMEM((n_row, seg, count, edge), f32),
            pltpu.VMEM((nz, seg, count, edge), f32),
            pltpu.VMEM((nz, seg, count, edge), f32),
            pltpu.VMEM((n_row, seg, count, edge), f32),
            pltpu.SemaphoreType.REGULAR, dma((2,)), dma((chunks,)), dma((4,)),
            dma((n_col,)), dma((n_col,)), dma((n_row,)), dma((n_row,)), dma, dma,
            dma((nz,)), dma((nz,)), dma((n_row,)), dma((n_row,)),
        ],
        compiler_params=pltpu.CompilerParams(
            collective_id=0, has_side_effects=True, vmem_limit_bytes=60 * 1024 * 1024),
        cost_estimate=pl.CostEstimate(
            flops=4 * slots * count * edge * edge, bytes_accessed=2 * slots * edge * edge, transcendentals=0),
    )(vectors, blocks, row_ptr, col_idx)


def solution(mesh):
    in_specs = (
        P(None, ("row", "col")),
        P("row", "col", None, None),
        P("row", "col"),
        P("row", "col"),
    )
    out_specs = P(None, ("row", "col"))
    shape = dict(mesh.shape)
    return jax.shard_map(
        functools.partial(body, shape["row"], shape["col"]),
        mesh=mesh, in_specs=in_specs, out_specs=out_specs, check_vma=False)
```

```python
import functools
import math

import jax
import jax.numpy as jnp
from jax import lax
from jax.experimental import pallas as pl
from jax.experimental.pallas import tpu as pltpu
from jax.sharding import PartitionSpec as P

MESH = pl.DeviceIdType.MESH
GROUP = 48
FAR = 1 << 20


def slot_tables(pointers, columns, tile_cols):
    slots = columns.shape[1]
    tile_rows = pointers.shape[1] - 1
    i32 = jnp.int32

    def iota(shape, dim):
        return lax.broadcasted_iota(i32, shape, dim)

    def total(mask_or_value, axis):
        return jnp.sum(mask_or_value, axis=axis, keepdims=True)

    def count(mask, axis):
        return total(jnp.where(mask, 1, 0), axis)

    corner = (tile_rows + 1, tile_rows + 1)
    pointer_col = total(jnp.where(iota(corner, 0) == iota(corner, 1), pointers, 0), 1)
    wide = (tile_rows + 1, slots)
    rows = count(pointer_col <= iota(wide, 1), 0) - 1
    keep_row = jnp.where(count(pointer_col == iota(wide, 1), 0) == 0, 1, 0)

    square = (slots, slots)
    lane, sub = iota(square, 1), iota(square, 0)
    slot_row = iota((1, slots), 1)
    key = jnp.where(rows < tile_rows, columns * slots, FAR) + slot_row
    rows = jnp.minimum(rows, tile_rows - 1)
    same = lane == sub
    key_col = total(jnp.where(same, key, 0), 1)
    rows_col = total(jnp.where(same, rows, 0), 1)
    rank_col = count(key < key_col, 1)
    chosen = rank_col == lane
    order = total(jnp.where(chosen, sub, 0), 0)
    order_rows = total(jnp.where(chosen, rows_col, 0), 0)
    tall = (tile_cols, slots)
    ends_col = count(key < (iota(tall, 0) + 1) * slots, 1)
    starts = count(ends_col == iota(tall, 1), 0)
    keep_col = jnp.where((starts == 0) & (slot_row > 0), 1, 0)
    side = (tile_cols, tile_cols)
    ends = total(jnp.where(iota(side, 0) == iota(side, 1), ends_col, 0), 0)
    return keep_row, order, order_rows, keep_col, ends


def kernel(
    n_row, n_col, chunks, group,
    vec_hbm, blk_hbm, ptr_hbm, col_hbm, out_ref,
    blk, ptr_s, col_s, ptr_v, col_v, table_v, table_s,
    row_side, col_side, row_blocks, col_blocks, run, fwd, bwd, near, fwd_in, bwd_in,
    here, vec_sem, blk_sem, idx_sem,
    rs_send, rs_recv, relay_send, cs_send, cs_recv, near_send, near_recv,
    f_send, f_recv, b_send, b_recv,
):
    r = lax.axis_index("row")
    c = lax.axis_index("col")
    z, core = c // 2, c % 2
    nz = n_col // 2
    sibling = z * 2 + 1 - core
    edge = blk.shape[1]
    seg = vec_hbm.shape[1] // edge
    slots = blk.shape[0]
    per = slots // chunks
    f32 = jnp.float32

    own_copies = [
        pltpu.make_async_copy(vec_hbm, dst, vec_sem.at[k])
        for k, dst in enumerate((col_side.at[r], row_side.at[c]))
    ]
    for copy in own_copies:
        copy.start()

    barrier = pltpu.get_barrier_semaphore()

    @pl.loop(1, n_row)
    def _(d):
        pl.semaphore_signal(barrier, inc=1, device_id=((r + d) % n_row, c), device_id_type=MESH)

    @pl.loop(c + 1, n_col)
    def _(p):
        pl.semaphore_signal(barrier, inc=1, device_id=(r, p), device_id_type=MESH)

    index_copies = [
        pltpu.make_async_copy(src, dst, idx_sem.at[k])
        for k, (src, dst) in enumerate(
            ((ptr_hbm, ptr_v), (col_hbm, col_v), (ptr_hbm, ptr_s), (col_hbm, col_s))
        )
    ]
    for copy in index_copies:
        copy.start()

    def chunk_copy(k):
        part = pl.ds(k * per, per)
        return pltpu.make_async_copy(blk_hbm.at[0, part], blk.at[part], blk_sem.at[k])

    for copy in own_copies:
        copy.wait()
    pl.semaphore_wait(barrier, n_row - 1 + c)

    def cs_copy(d, mine):
        owner = r if mine else (r + n_row - d) % n_row
        return pltpu.make_async_remote_copy(
            src_ref=col_side.at[r], dst_ref=col_side.at[owner],
            send_sem=cs_send.at[d], recv_sem=cs_recv.at[d],
            device_id=((r + d) % n_row, c), device_id_type=MESH)

    def rs_copy(to, source):
        return pltpu.make_async_remote_copy(
            src_ref=row_side.at[c], dst_ref=row_side.at[source],
            send_sem=rs_send.at[to], recv_sem=rs_recv.at[source],
            device_id=(r, to), device_id_type=MESH)

    def relay(source):
        return pltpu.make_async_remote_copy(
            src_ref=row_side.at[source], dst_ref=row_side.at[source],
            send_sem=relay_send.at[source], recv_sem=rs_recv.at[source],
            device_id=(r, sibling), device_id_type=MESH)

    @pl.loop(1, n_row)
    def _(d):
        cs_copy(d, True).start()

    @pl.loop(0, c)
    def _(p):
        pl.semaphore_signal(here, inc=1, device_id=(r, p), device_id_type=MESH)

    @pl.loop(0, z)
    def _(p):
        rs_copy(p * 2 + core, c).start()

    @pl.when(core == 1)
    def _():
        rs_copy(sibling, c).start()

    for k in range(chunks):
        chunk_copy(k).start()

    for copy in index_copies:
        copy.wait()
    table_v[...] = jnp.zeros_like(table_v)
    tables = slot_tables(ptr_v[...], col_v[...], n_row * seg)
    for k, entry in enumerate(tables):
        table_v[k:k + 1, 0:entry.shape[1]] = entry
    put_table = pltpu.make_async_copy(table_v, table_s, idx_sem.at[0])
    put_table.start()
    run[slots] = jnp.zeros(run.shape[1:], f32)
    put_table.wait()

    @pl.loop(1, n_row)
    def _(d):
        cs_copy(d, False).wait_recv()

    def side_by_side(sides, tiles, across):
        left = jnp.concatenate(sides, 0)
        right = jnp.concatenate(tiles, 1 - across)
        out = lax.dot_general(left, right, (((1,), (across,)), ((), ())), preferred_element_type=f32)
        m, n = sides[0].shape
        return [out[k * m:(k + 1) * m, k * n:(k + 1) * n] for k in range(len(sides))]

    step = math.gcd(group, 2)

    def group_loop(side_of, tile_of, keep_row, across):
        def one_group(g, total):
            for j in range(0, group, step):
                ids = [g * group + j + k for k in range(step)]
                terms = side_by_side([side_of(s) for s in ids], [tile_of(s) for s in ids], across)
                for s, term in zip(ids, terms):
                    total = total * table_s[keep_row, s].astype(f32) + term
                    run[s] = total
            return total
        return one_group

    def split(side, out, owners):
        @pl.loop(0, owners)
        def _(p):
            for u in range(seg):
                out[p * seg + u] = side[p, :, u * edge:(u + 1) * edge]

    forward_group = group_loop(lambda s: col_blocks[col_s[0, s]], lambda s: blk[s], 0, 1)
    backward_group = group_loop(
        lambda s: row_blocks[table_s[2, s]], lambda s: blk[table_s[1, s]], 3, 0)

    split(col_side, col_blocks, n_row)

    def forward_step(g, total):
        @pl.when(g == chunks // 2)
        def _():
            @pl.when(c < n_col - 1)
            def _():
                pl.semaphore_wait(here, n_col - 1 - c)

            @pl.loop(z + 1, nz)
            def _(p):
                rs_copy(p * 2 + core, c).start()

            @pl.when(core == 0)
            def _():
                rs_copy(sibling, c).start()

        @pl.when(g == chunks - 1)
        def _():
            @pl.loop(1, nz)
            def _(d):
                p = (z + nz - d) % nz * 2 + core
                rs_copy(p, p).wait_recv()
                relay(p).start()

        chunk_copy(g).wait()
        return forward_group(g, total)

    lax.fori_loop(0, chunks, forward_step, jnp.zeros(run.shape[1:], f32))

    @pl.loop(0, n_col)
    def _(p):
        for u in range(seg):
            first, last = ptr_s[0, p * seg + u], ptr_s[0, p * seg + u + 1]
            fwd[p % 2, p // 2, u] = run[jnp.where(last > first, last - 1, slots)]

    near_copy = pltpu.make_async_remote_copy(
        src_ref=fwd.at[1 - core], dst_ref=near, send_sem=near_send, recv_sem=near_recv,
        device_id=(r, z * 2 + 1 - core), device_id_type=MESH)
    near_copy.start()

    @pl.loop(0, nz)
    def _(d):
        p = (z + d) % nz * 2 + 1 - core
        rs_copy(p, p).wait_recv()

    split(row_side, row_blocks, n_col)

    def f_copy(d, mine):
        to = (z + d) % nz
        return pltpu.make_async_remote_copy(
            src_ref=fwd.at[core, to], dst_ref=fwd_in.at[z if mine else (z + nz - d) % nz],
            send_sem=f_send.at[d], recv_sem=f_recv.at[d],
            device_id=(r, to * 2 + core), device_id_type=MESH)

    def backward_step(g, total):
        @pl.when(g == max(chunks // 4, 1))
        def _():
            near_copy.wait()

            @pl.loop(0, nz)
            def _(p):
                fwd[core, p] = fwd[core, p] + near[p]

            @pl.loop(1, nz)
            def _(d):
                f_copy(d, True).start()

        return backward_group(g, total)

    lax.fori_loop(0, chunks, backward_step, jnp.zeros(run.shape[1:], f32))

    @pl.loop(0, n_row)
    def _(p):
        for u in range(seg):
            q = p * seg + u
            last = table_s[4, q]
            first = jnp.where(q > 0, table_s[4, jnp.maximum(q - 1, 0)], 0)
            bwd[p, u] = run[jnp.where(last > first, last - 1, slots)]

    def b_copy(d, mine):
        to = (r + d) % n_row
        return pltpu.make_async_remote_copy(
            src_ref=bwd.at[to], dst_ref=bwd_in.at[r if mine else (r + n_row - d) % n_row],
            send_sem=b_send.at[d], recv_sem=b_recv.at[d],
            device_id=(to, c), device_id_type=MESH)

    @pl.loop(1, n_row)
    def _(d):
        b_copy(d, True).start()

    bwd_in[r] = bwd[r]
    fwd_in[z] = fwd[core, z]

    @pl.loop(1, nz)
    def _(d):
        f_copy(d, False).wait_recv()

    parts = [fwd_in[p] for p in range(nz)]

    @pl.loop(1, n_row)
    def _(d):
        b_copy(d, False).wait_recv()

    parts = parts + [bwd_in[p] for p in range(n_row)]
    result = functools.reduce(lambda a, b: a + b, parts)
    for u in range(seg):
        out_ref[:, u * 128:(u + 1) * 128] = result[u]

    @pl.loop(1, n_row)
    def _(d):
        cs_copy(d, True).wait_send()
        b_copy(d, True).wait_send()

    rs_copy(sibling, c).wait_send()

    @pl.loop(1, nz)
    def _(d):
        p = (z + d) % nz * 2 + core
        rs_copy(p, c).wait_send()
        relay(p).wait_send()

    @pl.loop(1, nz)
    def _(d):
        f_copy(d, True).wait_send()


def body(n_row, n_col, vectors, blocks, row_ptr, col_idx):
    count, segment = vectors.shape
    slots, edge = blocks.shape[1], blocks.shape[2]
    seg = segment // edge
    group = math.gcd(slots, GROUP)
    chunks = slots // group
    i32, f32, bf16 = jnp.int32, jnp.float32, jnp.bfloat16
    width = -(-max(slots, n_row * seg) // 128) * 128
    nz = n_col // 2
    dma = pltpu.SemaphoreType.DMA
    anywhere = pl.BlockSpec(memory_space=pltpu.HBM)
    return pl.pallas_call(
        functools.partial(kernel, n_row, n_col, chunks, group),
        out_shape=jax.ShapeDtypeStruct((count, segment), f32),
        in_specs=[anywhere] * 4,
        out_specs=pl.BlockSpec(memory_space=pltpu.VMEM),
        scratch_shapes=[
            pltpu.VMEM((slots, edge, edge), bf16),
            pltpu.SMEM(row_ptr.shape, i32),
            pltpu.SMEM(col_idx.shape, i32),
            pltpu.VMEM(row_ptr.shape, i32),
            pltpu.VMEM(col_idx.shape, i32),
            pltpu.VMEM((8, width), i32),
            pltpu.SMEM((8, width), i32),
            pltpu.VMEM((n_col, count, segment), bf16),
            pltpu.VMEM((n_row, count, segment), bf16),
            pltpu.VMEM((n_col * seg, count, edge), bf16),
            pltpu.VMEM((n_row * seg, count, edge), bf16),
            pltpu.VMEM((slots + 1, count, edge), f32),
            pltpu.VMEM((2, nz, seg, count, edge), f32),
            pltpu.VMEM((n_row, seg, count, edge), f32),
            pltpu.VMEM((nz, seg, count, edge), f32),
            pltpu.VMEM((nz, seg, count, edge), f32),
            pltpu.VMEM((n_row, seg, count, edge), f32),
            pltpu.SemaphoreType.REGULAR, dma((2,)), dma((chunks,)), dma((4,)),
            dma((n_col,)), dma((n_col,)), dma((n_col,)), dma((n_row,)), dma((n_row,)), dma, dma,
            dma((nz,)), dma((nz,)), dma((n_row,)), dma((n_row,)),
        ],
        compiler_params=pltpu.CompilerParams(
            collective_id=0, has_side_effects=True, vmem_limit_bytes=60 * 1024 * 1024),
        cost_estimate=pl.CostEstimate(
            flops=4 * slots * count * edge * edge, bytes_accessed=2 * slots * edge * edge, transcendentals=0),
    )(vectors, blocks, row_ptr, col_idx)


def solution(mesh):
    in_specs = (
        P(None, ("row", "col")),
        P("row", "col", None, None),
        P("row", "col"),
        P("row", "col"),
    )
    out_specs = P(None, ("row", "col"))
    shape = dict(mesh.shape)
    return jax.shard_map(
        functools.partial(body, shape["row"], shape["col"]),
        mesh=mesh, in_specs=in_specs, out_specs=out_specs, check_vma=False)
```
